256 devices in a mesh: row: 16 (over x, z_hi), col: 16 (over z_lo, y, core).
Axes of the slice: x: 4, y: 4, z: 8 (z_hi: 4, z_lo: 2; z = z_hi * 2 + z_lo), core: 2. Of those that a mesh axis runs over, the one named last changes fastest.
Arguments:
- row_locs: float32 [2, 32768], P(None, 'row'), may hold values from 0 to 1
- panel_locs: float32 [2, 512], replicated, may hold values from 0 to 1
- prior_panel: float32 [32768, 512], P('row', 'col'), may hold values from -0.625 to 0.625
- prior_trail: float32 [32768, 8192], P('row', 'col'), may hold values from -1.25 to 1.25
Outputs:
- panel_factor: float32 [32768, 512], P('row')
- trailing: float32 [32768, 8192], P('row', 'col')
The draws below stay inside these ranges and needn't reach their ends.
All inputs are finite; a program needn't handle non-finite values.
Results may differ from the reference program's by a relative error of at most 0.0003.
Values sent between devices are 32-bit elements; how exact they have to be, the bound alone decides.
A program may use at most 64 MiB of HBM per device.

```python
import jax
import jax.numpy as jnp
from jax import lax

NB = 512
RT_DEV = 4
ROWS = 32768
COLS = 8192
N_ROW = 16
N_COL = 16


def block_levels(own_key, dims, split, smallest, top_value):
    factor_of, own = 1.0, jax.random.fold_in(own_key, 6)
    for position, parts in split:
        heights = jnp.exp(jax.random.uniform(jax.random.fold_in(own, position), (parts,), jnp.float32, smallest / len(split), top_value / len(split)))
        factor_of = factor_of * jnp.repeat(heights, dims[position] // parts).reshape([-1 if axis == position else 1 for axis in range(len(dims))])
    return factor_of


def centred(stream_key, dims, deviation, reach, split=(), held_as=jnp.bfloat16):
    drawn = deviation * jax.random.normal(stream_key, dims, jnp.float32)
    if split:
        drawn = drawn * block_levels(stream_key, dims, split, -0.22, 0.18)
    return jnp.clip(drawn, -reach, reach).astype(held_as)


def setup_inputs(seed: int = 0) -> dict:
    seeds = jax.random.split(jax.random.key(seed), 5)
    return {
        "row_locs": jnp.clip(1.0 * jax.random.uniform(seeds[0], (2, ROWS), jnp.float32) ** block_levels(seeds[0], (2, ROWS), ((1, 16),), -0.2, 0.2), 0.0, 1.0),
        "panel_locs": jnp.clip(jax.random.uniform(seeds[1], (2, NB), jnp.float32, 0.0, 1.0), 0.0, 1.0),
        "prior_panel": centred(seeds[2], (ROWS, NB), 0.1, 0.625, ((0, 16), (1, 16)), jnp.float32),
        "prior_trail": centred(seeds[3], (ROWS, COLS), 0.2, 1.25, ((0, 16), (1, 16)), jnp.float32),
    }


corr_range = 0.1
nugget_value = 0.1

def kernel(left_locs, right_locs):
    delta_x = left_locs[0][:, None] - right_locs[0][None, :]
    delta_y = left_locs[1][:, None] - right_locs[1][None, :]
    return jnp.exp(-jnp.sqrt(delta_x * delta_x + delta_y * delta_y) / corr_range)

def times_inverse(tiles, inv_lower):
    return lax.dot_general(tiles.astype(jnp.float32), inv_lower.astype(jnp.float32), (((1,), (1,)), ((), ())), precision=lax.Precision.HIGHEST, preferred_element_type=jnp.float32)

def reference(row_locs, panel_locs, prior_panel, prior_trail):
    identity = jnp.eye(NB, dtype=jnp.float32)
    diag_tile = kernel(panel_locs, panel_locs) + nugget_value * identity
    lower_factor = jnp.linalg.cholesky(diag_tile)
    inv_lower = jax.scipy.linalg.solve_triangular(lower_factor, identity, lower=True)
    panel_tiles = kernel(row_locs, panel_locs) - prior_panel
    panel_factor = times_inverse(panel_tiles, inv_lower)
    rows_dev = RT_DEV * NB
    col_locs = row_locs.reshape(2, N_ROW, rows_dev)[:, :N_COL, :NB].reshape(2, N_COL * NB)
    col_factor = panel_factor.reshape(N_ROW, rows_dev, NB)[:N_COL, :NB].reshape(N_COL * NB, NB)
    col_index = (jnp.arange(N_COL, dtype=jnp.int32)[:, None] * rows_dev + jnp.arange(NB, dtype=jnp.int32)[None, :]).reshape(N_COL * NB)
    block_count = ROWS // NB

    def one_block(block_id):
        first_row = (block_id * NB).astype(jnp.int32)
        locs_block = lax.dynamic_slice_in_dim(row_locs, first_row, NB, 1)
        factor_block = lax.dynamic_slice_in_dim(panel_factor, first_row, NB, 0)
        prior_block = lax.dynamic_slice_in_dim(prior_trail, first_row, NB, 0)
        row_index = first_row + jnp.arange(NB, dtype=jnp.int32)
        same_point = (row_index[:, None] == col_index[None, :]).astype(jnp.float32)
        kernel_block = kernel(locs_block, col_locs) + nugget_value * same_point
        update = lax.dot_general(factor_block.astype(jnp.float32), col_factor.astype(jnp.float32), (((1,), (1,)), ((), ())), precision=lax.Precision.HIGHEST, preferred_element_type=jnp.float32)
        return kernel_block - prior_block - update
    trailing = lax.map(one_block, jnp.arange(block_count, dtype=jnp.int32)).reshape(ROWS, N_COL * NB)
    return (panel_factor, trailing)
```

```python
import jax
import jax.numpy as jnp
from jax import lax
from jax.experimental import pallas as pl
from jax.experimental.pallas import tpu as pltpu
from jax.sharding import PartitionSpec as P

STRIP = 16
BLOCK = 128
f32, bf16 = jnp.float32, jnp.bfloat16


def exp_distance(dx, dy):
    d2 = dx * dx + dy * dy
    return jnp.exp(d2 * lax.rsqrt(jnp.maximum(d2, 1e-30)) * -10.0)


def split3(x):
    a = x.astype(bf16)
    r = x - a.astype(f32)
    b = r.astype(bf16)
    return a, b, (r - b.astype(f32)).astype(bf16)


def lanes_of(x, j):
    return jnp.broadcast_to(x[:, j : j + 1], (8, BLOCK))


def row_of(x, i):
    return jnp.broadcast_to(x[i : i + 1, :], (8, BLOCK))


def invert_block(d_ref):
    lane = lax.broadcasted_iota(jnp.int32, (8, BLOCK), 1)
    sub = lax.broadcasted_iota(jnp.int32, (8, BLOCK), 0)
    groups = STRIP // 8
    for strip in range(BLOCK // STRIP):
        base = strip * STRIP
        rows = [d_ref[base + 8 * g : base + 8 * g + 8, :] for g in range(groups)]
        cols = [[lanes_of(rows[g], base + j) for g in range(groups)] for j in range(STRIP)]
        scale = [jnp.zeros((8, BLOCK), f32)] * groups
        for i in range(STRIP):
            h, q = i // 8, i % 8
            pivot = row_of(cols[i][h], q)
            inv_pivot = 1.0 / pivot
            scale[h] = jnp.where(sub == q, lax.rsqrt(pivot), scale[h])
            f = [None] * groups
            f[h] = jnp.where(sub > q, cols[i][h], 0.0) * inv_pivot
            for g in range(h + 1, groups):
                f[g] = cols[i][g] * inv_pivot
            for j in range(i + 1, STRIP):
                t = row_of(cols[j][h], q)
                for g in range(h, groups):
                    cols[j][g] = cols[j][g] - f[g] * t
            rows[h] = jnp.where(lane == base + i, jnp.where(sub == q, 1.0, 0.0), rows[h])
            for g in range(h + 1, groups):
                rows[g] = jnp.where(lane == base + i, 0.0, rows[g])
            t = row_of(rows[h], q)
            for g in range(h, groups):
                rows[g] = rows[g] - f[g] * t
        for g in range(groups):
            above = (lane > base + 8 * g + sub) & (lane < base + STRIP)
            rows[g] = jnp.where(above, 0.0, rows[g]) * scale[g]
            d_ref[base + 8 * g : base + 8 * g + 8, :] = rows[g]
        first = base + STRIP
        if first < BLOCK:
            a, b, c = split3(jnp.concatenate(rows, axis=0))
            left = jnp.concatenate([a, a, b, a, b, c], axis=0)
            right = jnp.concatenate([a, b, a, c, b, a], axis=0)
            update = lax.dot_general(left, right, (((0,), (0,)), ((), ())), preferred_element_type=f32)
            wide = lax.broadcasted_iota(jnp.int32, (BLOCK - first, BLOCK), 1)
            old = jnp.where((wide >= base) & (wide < first), 0.0, d_ref[first:, :])
            d_ref[first:, :] = old - update[first:, :]


def hdot(a, b, dims):
    return lax.dot_general(a, b, (dims, ((), ())), precision=lax.Precision.HIGHEST, preferred_element_type=f32)


def fill_matrix(locs_ref, m_ref, n):
    blocks = n // BLOCK
    eye = lax.broadcasted_iota(jnp.int32, (BLOCK, BLOCK), 0) == lax.broadcasted_iota(jnp.int32, (BLOCK, BLOCK), 1)
    for bi in range(blocks):
        col = [jnp.transpose(jnp.broadcast_to(locs_ref[c : c + 1, bi * BLOCK : (bi + 1) * BLOCK], (BLOCK, BLOCK))) for c in (0, 1)]
        for bj in range(blocks):
            at = (slice(bi * BLOCK, (bi + 1) * BLOCK), slice(bj * BLOCK, (bj + 1) * BLOCK))
            if bj < bi:
                m_ref[at] = jnp.zeros((BLOCK, BLOCK), f32)
                continue
            row = [locs_ref[c : c + 1, bj * BLOCK : (bj + 1) * BLOCK] for c in (0, 1)]
            value = exp_distance(col[0] - row[0], col[1] - row[1])
            if bi == bj:
                value = value + jnp.where(eye, 0.1, 0.0)
            m_ref[at] = value


def chol_kernel(locs_ref, inv_ref, m_ref, d_ref):
    n = locs_ref.shape[1]
    blocks = n // BLOCK
    fill_matrix(locs_ref, m_ref, n)
    lower = lax.broadcasted_iota(jnp.int32, (BLOCK, BLOCK), 0) >= lax.broadcasted_iota(jnp.int32, (BLOCK, BLOCK), 1)
    lane_block = lax.broadcasted_iota(jnp.int32, (BLOCK, n), 1) // BLOCK

    def one_block(k, carry):
        mine = pl.ds(pl.multiple_of(k * BLOCK, BLOCK), BLOCK)
        d_ref[...] = m_ref[mine, mine]
        invert_block(d_ref)
        w = jnp.where(lower, d_ref[...], 0.0)
        row = hdot(w, m_ref[mine, :], ((1,), (0,)))
        m_ref[mine, :] = row
        m_ref[mine, mine] = w
        row = m_ref[mine, :]
        inv_ref[mine, :] = jnp.where(lane_block <= k, row, 0.0)

        def below(i, carry):
            his = pl.ds(pl.multiple_of(i * BLOCK, BLOCK), BLOCK)
            update = hdot(m_ref[mine, his], row, ((0,), (0,)))
            m_ref[his, :] = jnp.where(lane_block == k, 0.0, m_ref[his, :]) - update
            return carry

        return lax.fori_loop(k + 1, blocks, below, carry)

    lax.fori_loop(0, blocks, one_block, 0)


def invert_factor(locs):
    n = locs.shape[1]
    return pl.pallas_call(
        chol_kernel,
        out_shape=jax.ShapeDtypeStruct((n, n), f32),
        in_specs=[pl.BlockSpec(memory_space=pltpu.VMEM)],
        out_specs=pl.BlockSpec(memory_space=pltpu.VMEM),
        scratch_shapes=[pltpu.VMEM((n, n), f32), pltpu.VMEM((BLOCK, BLOCK), f32)],
        compiler_params=pltpu.CompilerParams(vmem_limit_bytes=32 * 2**20),
        cost_estimate=pl.CostEstimate(flops=2 * n**3, bytes_accessed=8 * n * n, transcendentals=n * n),
        name="invert_factor",
    )(locs)


ROW_TILE = 256


def split2(x):
    high = x.astype(bf16)
    return high, (x - high.astype(f32)).astype(bf16)


def dot3(left, right):
    def one(a, b):
        return lax.dot_general(a, b, (((1,), (1,)), ((), ())), preferred_element_type=f32)

    return one(left[0], right[0]) + (one(left[0], right[1]) + one(left[1], right[0]))


def across(row):
    return jnp.transpose(jnp.broadcast_to(row, (BLOCK, BLOCK)))


def trailing_kernel(panel_ref, tile_ref, inv_ref, row_locs_ref, col_locs_ref, prior_ref, factor_ref, out_ref, inv_h, inv_l, col_h, col_l):
    step = pl.program_id(0)
    width = out_ref.shape[1]

    @pl.when(step == 0)
    def _():
        high, low = split2(inv_ref[...])
        inv_h[...] = high
        inv_l[...] = low
        col_factor = dot3(split2(jnp.transpose(tile_ref[...])), (high, low))
        col_h[...], col_l[...] = split2(col_factor)

    factor = dot3(split2(jnp.transpose(panel_ref[...])), (inv_h[...], inv_l[...]))
    factor_ref[...] = factor
    update = dot3(split2(factor), (col_h[...], col_l[...]))
    on_diagonal = lax.axis_index("row") == lax.axis_index("col")
    for part in range(ROW_TILE // BLOCK):
        rows = slice(part * BLOCK, (part + 1) * BLOCK)
        xr = across(row_locs_ref[0:1, rows])
        yr = across(row_locs_ref[1:2, rows])
        for block in range(width // BLOCK):
            cols = slice(block * BLOCK, (block + 1) * BLOCK)
            value = exp_distance(xr - col_locs_ref[0:1, cols], yr - col_locs_ref[1:2, cols])
            i = lax.broadcasted_iota(jnp.int32, (BLOCK, BLOCK), 0) + (step * ROW_TILE + part * BLOCK)
            j = lax.broadcasted_iota(jnp.int32, (BLOCK, BLOCK), 1) + block * BLOCK
            value = value + jnp.where((i == j) & on_diagonal, 0.1, 0.0)
            out_ref[rows, cols] = value - prior_ref[rows, cols] - update[rows, cols]


def trailing_update(panel_t, tile_t, inv_lower, row_locs, col_locs, prior_trail):
    depth, rows = panel_t.shape
    width = prior_trail.shape[1]
    whole = lambda shape: pl.BlockSpec(shape, lambda i: (0, 0))
    return pl.pallas_call(
        trailing_kernel,
        grid=(rows // ROW_TILE,),
        out_shape=(jax.ShapeDtypeStruct((rows, depth), f32), jax.ShapeDtypeStruct((rows, width), f32)),
        in_specs=[
            pl.BlockSpec((depth, ROW_TILE), lambda i: (0, i)),
            whole((depth, width)),
            whole((depth, depth)),
            pl.BlockSpec((2, ROW_TILE), lambda i: (0, i)),
            whole((2, width)),
            pl.BlockSpec((ROW_TILE, width), lambda i: (i, 0)),
        ],
        out_specs=(pl.BlockSpec((ROW_TILE, depth), lambda i: (i, 0)), pl.BlockSpec((ROW_TILE, width), lambda i: (i, 0))),
        scratch_shapes=[pltpu.VMEM((depth, depth), bf16)] * 2 + [pltpu.VMEM((width, depth), bf16)] * 2,
        compiler_params=pltpu.CompilerParams(vmem_limit_bytes=60 * 2**20),
        cost_estimate=pl.CostEstimate(flops=12 * rows * depth * width, bytes_accessed=16 * rows * width, transcendentals=2 * rows * width),
        name="trailing_update",
    )(panel_t, tile_t, inv_lower, row_locs, col_locs, prior_trail)


def covariance(left_locs, right_locs):
    return exp_distance(left_locs[0][:, None] - right_locs[0][None, :], left_locs[1][:, None] - right_locs[1][None, :])


def body(row_locs, panel_locs, prior_panel, prior_trail):
    tile = panel_locs.shape[1]
    width = prior_panel.shape[1]
    n = lax.axis_size("col")
    my_panel_locs = lax.dynamic_slice_in_dim(panel_locs, lax.axis_index("col") * width, width, 1)
    part = covariance(my_panel_locs, row_locs) - prior_panel.T
    swap = [(r * n + c, c * n + r) for r in range(n) for c in range(n)]
    packed = jnp.concatenate([part[:, :tile], row_locs[:, :tile], jnp.zeros((6, tile), f32)], axis=0)
    packed = lax.ppermute(packed, ("row", "col"), swap)
    tile_t = lax.all_gather(packed[:width], "row", axis=0, tiled=True)
    panel_t = lax.all_gather(part, "col", axis=0, tiled=True)
    inv_lower = invert_factor(panel_locs)
    return trailing_update(panel_t, tile_t, inv_lower, row_locs, packed[width : width + 2], prior_trail)


def solution(mesh):
    in_specs = (P(None, "row"), P(), P("row", "col"), P("row", "col"))
    out_specs = (P("row", None), P("row", "col"))
    return jax.shard_map(body, mesh=mesh, in_specs=in_specs, out_specs=out_specs, check_vma=False)
```

```python
import jax
import jax.numpy as jnp
from jax import lax
from jax.experimental import pallas as pl
from jax.experimental.pallas import tpu as pltpu
from jax.sharding import PartitionSpec as P

STRIP = 16
BLOCK = 128
VMEM_A = 60 * 2**20
f32, bf16 = jnp.float32, jnp.bfloat16


def exp_distance(dx, dy):
    d2 = dx * dx + dy * dy
    return jnp.exp(d2 * lax.rsqrt(jnp.maximum(d2, 1e-30)) * -10.0)


def split3(x):
    a = x.astype(bf16)
    r = x - a.astype(f32)
    b = r.astype(bf16)
    return a, b, (r - b.astype(f32)).astype(bf16)


def lanes_of(x, j):
    return jnp.broadcast_to(x[:, j : j + 1], (8, BLOCK))


def row_of(x, i):
    return jnp.broadcast_to(x[i : i + 1, :], (8, BLOCK))


def invert_block(d_ref):
    lane = lax.broadcasted_iota(jnp.int32, (8, BLOCK), 1)
    sub = lax.broadcasted_iota(jnp.int32, (8, BLOCK), 0)
    groups = STRIP // 8
    for strip in range(BLOCK // STRIP):
        base = strip * STRIP
        rows = [d_ref[base + 8 * g : base + 8 * g + 8, :] for g in range(groups)]
        cols = [[lanes_of(rows[g], base + j) for g in range(groups)] for j in range(STRIP)]
        scale = [jnp.zeros((8, BLOCK), f32)] * groups
        for i in range(STRIP):
            h, q = i // 8, i % 8
            pivot = row_of(cols[i][h], q)
            inv_pivot = 1.0 / pivot
            scale[h] = jnp.where(sub == q, lax.rsqrt(pivot), scale[h])
            f = [None] * groups
            f[h] = jnp.where(sub > q, cols[i][h], 0.0) * inv_pivot
            for g in range(h + 1, groups):
                f[g] = cols[i][g] * inv_pivot
            for j in range(i + 1, STRIP):
                t = row_of(cols[j][h], q)
                for g in range(h, groups):
                    cols[j][g] = cols[j][g] - f[g] * t
            rows[h] = jnp.where(lane == base + i, jnp.where(sub == q, 1.0, 0.0), rows[h])
            for g in range(h + 1, groups):
                rows[g] = jnp.where(lane == base + i, 0.0, rows[g])
            t = row_of(rows[h], q)
            for g in range(h, groups):
                rows[g] = rows[g] - f[g] * t
        for g in range(groups):
            above = (lane > base + 8 * g + sub) & (lane < base + STRIP)
            rows[g] = jnp.where(above, 0.0, rows[g]) * scale[g]
            d_ref[base + 8 * g : base + 8 * g + 8, :] = rows[g]
        first = base + STRIP
        if first < BLOCK:
            a, b, c = split3(jnp.concatenate(rows, axis=0))
            left = jnp.concatenate([a, a, b, a, b, c], axis=0)
            right = jnp.concatenate([a, b, a, c, b, a], axis=0)
            update = lax.dot_general(left, right, (((0,), (0,)), ((), ())), preferred_element_type=f32)
            wide = lax.broadcasted_iota(jnp.int32, (BLOCK - first, BLOCK), 1)
            old = jnp.where((wide >= base) & (wide < first), 0.0, d_ref[first:, :])
            d_ref[first:, :] = old - update[first:, :]


def hdot(a, b, dims):
    return lax.dot_general(a, b, (dims, ((), ())), precision=lax.Precision.HIGHEST, preferred_element_type=f32)


def fill_matrix(locs_ref, m_ref, n):
    blocks = n // BLOCK
    eye = lax.broadcasted_iota(jnp.int32, (BLOCK, BLOCK), 0) == lax.broadcasted_iota(jnp.int32, (BLOCK, BLOCK), 1)
    for bi in range(blocks):
        col = [jnp.transpose(jnp.broadcast_to(locs_ref[c : c + 1, bi * BLOCK : (bi + 1) * BLOCK], (BLOCK, BLOCK))) for c in (0, 1)]
        for bj in range(blocks):
            at = (slice(bi * BLOCK, (bi + 1) * BLOCK), slice(bj * BLOCK, (bj + 1) * BLOCK))
            if bj < bi:
                m_ref[at] = jnp.zeros((BLOCK, BLOCK), f32)
                continue
            row = [locs_ref[c : c + 1, bj * BLOCK : (bj + 1) * BLOCK] for c in (0, 1)]
            value = exp_distance(col[0] - row[0], col[1] - row[1])
            if bi == bj:
                value = value + jnp.where(eye, 0.1, 0.0)
            m_ref[at] = value


ROW_TILE = 256


def split2(x):
    high = x.astype(bf16)
    return high, (x - high.astype(f32)).astype(bf16)


def dot3(left, right):
    def one(a, b):
        return lax.dot_general(a, b, (((1,), (1,)), ((), ())), preferred_element_type=f32)

    return one(left[0], right[0]) + (one(left[0], right[1]) + one(left[1], right[0]))


def across(row):
    return jnp.transpose(jnp.broadcast_to(row, (BLOCK, BLOCK)))


def trailing_kernel(panel_ref, tile_ref, inv_ref, row_locs_ref, col_locs_ref, prior_ref, factor_ref, out_ref, inv_h, inv_l, col_h, col_l):
    step = pl.program_id(0)
    width = out_ref.shape[1]

    @pl.when(step == 0)
    def _():
        high, low = split2(inv_ref[...])
        inv_h[...] = high
        inv_l[...] = low
        col_factor = dot3(split2(jnp.transpose(tile_ref[...])), (high, low))
        col_h[...], col_l[...] = split2(col_factor)

    factor = dot3(split2(jnp.transpose(panel_ref[...])), (inv_h[...], inv_l[...]))
    factor_ref[...] = factor
    update = dot3(split2(factor), (col_h[...], col_l[...]))
    on_diagonal = lax.axis_index("row") == lax.axis_index("col")
    for part in range(ROW_TILE // BLOCK):
        rows = slice(part * BLOCK, (part + 1) * BLOCK)
        xr = across(row_locs_ref[0:1, rows])
        yr = across(row_locs_ref[1:2, rows])
        for block in range(width // BLOCK):
            cols = slice(block * BLOCK, (block + 1) * BLOCK)
            value = exp_distance(xr - col_locs_ref[0:1, cols], yr - col_locs_ref[1:2, cols])
            i = lax.broadcasted_iota(jnp.int32, (BLOCK, BLOCK), 0) + (step * ROW_TILE + part * BLOCK)
            j = lax.broadcasted_iota(jnp.int32, (BLOCK, BLOCK), 1) + block * BLOCK
            value = value + jnp.where((i == j) & on_diagonal, 0.1, 0.0)
            out_ref[rows, cols] = value - prior_ref[rows, cols] - update[rows, cols]


def trailing_update(panel_t, tile_t, inv_lower, row_locs, col_locs, prior_trail):
    depth, rows = panel_t.shape
    width = prior_trail.shape[1]
    whole = lambda shape: pl.BlockSpec(shape, lambda i: (0, 0))
    return pl.pallas_call(
        trailing_kernel,
        grid=(rows // ROW_TILE,),
        out_shape=(jax.ShapeDtypeStruct((rows, depth), f32), jax.ShapeDtypeStruct((rows, width), f32)),
        in_specs=[
            pl.BlockSpec((depth, ROW_TILE), lambda i: (0, i)),
            whole((depth, width)),
            whole((depth, depth)),
            pl.BlockSpec((2, ROW_TILE), lambda i: (0, i)),
            whole((2, width)),
            pl.BlockSpec((ROW_TILE, width), lambda i: (i, 0)),
        ],
        out_specs=(pl.BlockSpec((ROW_TILE, depth), lambda i: (i, 0)), pl.BlockSpec((ROW_TILE, width), lambda i: (i, 0))),
        scratch_shapes=[pltpu.VMEM((depth, depth), bf16)] * 2 + [pltpu.VMEM((width, depth), bf16)] * 2,
        compiler_params=pltpu.CompilerParams(vmem_limit_bytes=60 * 2**20),
        cost_estimate=pl.CostEstimate(flops=12 * rows * depth * width, bytes_accessed=16 * rows * width, transcendentals=2 * rows * width),
        name="trailing_update",
    )(panel_t, tile_t, inv_lower, row_locs, col_locs, prior_trail)


MESH = pl.DeviceIdType.MESH


def invert_step(k, blocks, m_ref, d_ref, inv_ref):
    n = m_ref.shape[1]
    lower = lax.broadcasted_iota(jnp.int32, (BLOCK, BLOCK), 0) >= lax.broadcasted_iota(jnp.int32, (BLOCK, BLOCK), 1)
    lane_block = lax.broadcasted_iota(jnp.int32, (BLOCK, n), 1) // BLOCK
    mine = pl.ds(pl.multiple_of(k * BLOCK, BLOCK), BLOCK)
    d_ref[...] = m_ref[mine, mine]
    invert_block(d_ref)
    w = jnp.where(lower, d_ref[...], 0.0)
    m_ref[mine, :] = hdot(w, m_ref[mine, :], ((1,), (0,)))
    m_ref[mine, mine] = w
    row = m_ref[mine, :]
    inv_ref[mine, :] = jnp.where(lane_block <= k, row, 0.0)

    def below(i, carry):
        his = pl.ds(pl.multiple_of(i * BLOCK, BLOCK), BLOCK)
        update = hdot(m_ref[mine, his], row, ((0,), (0,)))
        m_ref[his, :] = jnp.where(lane_block == k, 0.0, m_ref[his, :]) - update
        return carry

    lax.fori_loop(k + 1, blocks, below, 0)


def gather_kernel(
    locs_ref, row_locs_ref, prior_ref,
    panel_ref, tile_ref, inv_ref, col_locs_ref,
    m_ref, d_ref, part_ref, turn_ref,
    panel_send, panel_recv, tile_send, tile_recv, swap_send, locs_recv, own_sem,
):
    n = locs_ref.shape[1]
    width, rows = prior_ref.shape
    tile = col_locs_ref.shape[1]
    blocks = n // BLOCK
    row, col = lax.axis_index("row"), lax.axis_index("col")
    x, z_hi = lax.div(row, 4), lax.rem(row, 4)
    z_lo, y, core = lax.div(col, 8), lax.rem(lax.div(col, 2), 4), lax.rem(col, 2)

    def col_of(a, b, c):
        return a * 8 + b * 2 + c

    sibling = col_of(z_lo, y, 1 - core)
    partner = col_of(1 - z_lo, y, core)
    y_cols = [col_of(z_lo, lax.rem(y + d, 4), core) for d in (1, 2, 3)]
    y_far = [col_of(1 - z_lo, lax.rem(y + d, 4), core) for d in (1, 2, 3)]
    z_rows = [x * 4 + lax.rem(z_hi + d, 4) for d in (1, 2, 3)]
    x_rows = [lax.rem(x + d, 4) * 4 + z_hi for d in (1, 2, 3)]

    barrier = pltpu.get_barrier_semaphore()
    for c in [sibling, partner] + y_cols:
        pl.semaphore_signal(barrier, inc=1, device_id=(row, c), device_id_type=MESH)
    for r in z_rows + x_rows:
        pl.semaphore_signal(barrier, inc=1, device_id=(r, col), device_id_type=MESH)

    @pl.when(row != col)
    def _():
        pl.semaphore_signal(barrier, inc=1, device_id=(col, row), device_id_type=MESH)

    at = pl.ds(pl.multiple_of(lax.div(col, 4) * BLOCK, BLOCK), BLOCK)
    mine = pl.ds(pl.multiple_of(lax.rem(col, 4) * width, width), width)
    for c in (0, 1):
        turn_ref[c] = across(locs_ref[c : c + 1, at])
    for b in range(rows // BLOCK):
        s = slice(b * BLOCK, (b + 1) * BLOCK)
        value = exp_distance(turn_ref[0, mine, :] - row_locs_ref[0:1, s], turn_ref[1, mine, :] - row_locs_ref[1:2, s])
        part_ref[:, s] = value - prior_ref[:, s]

    pl.semaphore_wait(barrier, jnp.where(row == col, 11, 12))

    def slice_of(c):
        return panel_ref.at[pl.ds(pl.multiple_of(c * width, width), width), :]

    def piece_of(r):
        return tile_ref.at[pl.ds(pl.multiple_of(r * width, width), width), :]

    def send(src, dst, send_sem, recv_sem, to):
        pltpu.make_async_remote_copy(src_ref=src, dst_ref=dst, send_sem=send_sem, recv_sem=recv_sem, device_id=to, device_id_type=MESH).start()

    def send_slice(src, c, slot, to_col):
        send(src, slice_of(c), panel_send.at[slot], panel_recv.at[c], (row, to_col))

    def send_piece(r, slot, to_row):
        send(piece_of(r), piece_of(r), tile_send.at[slot], tile_recv.at[r], (to_row, col))

    def arrived(ref, sem):
        pltpu.make_async_copy(ref, ref, sem).wait()

    own_copy = pltpu.make_async_copy(part_ref, slice_of(col), own_sem)
    swap_src = part_ref.at[:, 0:tile]
    locs_src = row_locs_ref.at[:, 0:tile]
    swap_copy = pltpu.make_async_remote_copy(src_ref=swap_src, dst_ref=piece_of(col), send_sem=swap_send.at[0], recv_sem=tile_recv.at[col], device_id=(col, row), device_id_type=MESH)
    locs_copy = pltpu.make_async_remote_copy(src_ref=locs_src, dst_ref=col_locs_ref, send_sem=swap_send.at[1], recv_sem=locs_recv, device_id=(col, row), device_id_type=MESH)

    send_slice(part_ref, col, 0, partner)

    @pl.when(row != col)
    def _():
        swap_copy.start()
        locs_copy.start()

    @pl.when(row == col)
    def _():
        pltpu.make_async_copy(swap_src, piece_of(row), tile_recv.at[row]).start()
        pltpu.make_async_copy(locs_src, col_locs_ref, locs_recv).start()

    for j in range(3):
        send_slice(part_ref, col, 1 + j, y_cols[j])
    send_slice(part_ref, col, 4, sibling)
    own_copy.start()

    fill_matrix(locs_ref, m_ref, n)

    def one_block(k, carry):
        invert_step(k, blocks, m_ref, d_ref, inv_ref)

        @pl.when(k == 0)
        def _():
            arrived(slice_of(partner), panel_recv.at[partner])
            for j in range(3):
                send_slice(slice_of(partner), partner, 5 + j, y_cols[j])
            send_slice(slice_of(partner), partner, 8, sibling)
            arrived(piece_of(row), tile_recv.at[row])
            for j in range(3):
                send_piece(row, j, z_rows[j])
                send_piece(row, 3 + j, x_rows[j])

        @pl.when(k == 1)
        def _():
            for j in range(3):
                arrived(piece_of(z_rows[j]), tile_recv.at[z_rows[j]])
                for i in range(3):
                    send_piece(z_rows[j], 6 + 3 * j + i, x_rows[i])

        @pl.when(k == 2)
        def _():
            for j in range(3):
                arrived(slice_of(y_cols[j]), panel_recv.at[y_cols[j]])
                send_slice(slice_of(y_cols[j]), y_cols[j], 9 + j, sibling)

        return carry

    lax.fori_loop(0, blocks, one_block, 0)

    for j in range(3):
        arrived(slice_of(y_far[j]), panel_recv.at[y_far[j]])
        send_slice(slice_of(y_far[j]), y_far[j], 12 + j, sibling)

    for a in range(2):
        for b in range(4):
            c = col_of(a, b, 1 - core)
            arrived(slice_of(c), panel_recv.at[c])
    for d in (1, 2, 3):
        for e in range(4):
            r = lax.rem(x + d, 4) * 4 + e
            arrived(piece_of(r), tile_recv.at[r])
    arrived(col_locs_ref, locs_recv)
    own_copy.wait()
    for slot in range(15):
        arrived(slice_of(col), panel_send.at[slot])
        arrived(piece_of(row), tile_send.at[slot])

    @pl.when(row != col)
    def _():
        swap_copy.wait_send()
        locs_copy.wait_send()


def gather_and_invert(panel_locs, row_locs, prior_t, tile):
    n = panel_locs.shape[1]
    width, rows = prior_t.shape
    n_col = n // width
    vmem = pl.BlockSpec(memory_space=pltpu.VMEM)
    anywhere = pl.BlockSpec(memory_space=pl.ANY)
    dma = pltpu.SemaphoreType.DMA
    return pl.pallas_call(
        gather_kernel,
        out_shape=(
            jax.ShapeDtypeStruct((n, rows), f32),
            jax.ShapeDtypeStruct((n, tile), f32),
            jax.ShapeDtypeStruct((n, n), f32),
            jax.ShapeDtypeStruct((2, tile), f32),
        ),
        in_specs=[vmem] * 3,
        out_specs=(anywhere, anywhere, vmem, vmem),
        scratch_shapes=[
            pltpu.VMEM((n, n), f32),
            pltpu.VMEM((BLOCK, BLOCK), f32),
            pltpu.VMEM((width, rows), f32),
            pltpu.VMEM((2, BLOCK, BLOCK), f32),
            dma((15,)), dma((n_col,)), dma((15,)), dma((n_col,)), dma((2,)), dma, dma,
        ],
        compiler_params=pltpu.CompilerParams(vmem_limit_bytes=VMEM_A, collective_id=0, has_side_effects=True),
        cost_estimate=pl.CostEstimate(flops=2 * n**3, bytes_accessed=8 * n * n, transcendentals=n * n),
        name="gather_and_invert",
    )(panel_locs, row_locs, prior_t)


def body(row_locs, panel_locs, prior_panel, prior_trail):
    tile = panel_locs.shape[1]
    panel_t, tile_t, inv_lower, col_locs = gather_and_invert(panel_locs, row_locs, prior_panel.T, tile)
    return trailing_update(panel_t, tile_t, inv_lower, row_locs, col_locs, prior_trail)


def solution(mesh):
    in_specs = (P(None, "row"), P(), P("row", "col"), P("row", "col"))
    out_specs = (P("row", None), P("row", "col"))
    return jax.shard_map(body, mesh=mesh, in_specs=in_specs, out_specs=out_specs, check_vma=False)
```

```python
import jax
import jax.numpy as jnp
from jax import lax
from jax.experimental import pallas as pl
from jax.experimental.pallas import tpu as pltpu
from jax.sharding import PartitionSpec as P

STRIP = 16
BLOCK = 128
VMEM_A = 24 * 2**20
VMEM_B = 24 * 2**20
f32, bf16 = jnp.float32, jnp.bfloat16


def exp_distance(dx, dy):
    d2 = dx * dx + dy * dy
    return jnp.exp(d2 * lax.rsqrt(jnp.maximum(d2, 1e-30)) * -10.0)


def split3(x):
    a = x.astype(bf16)
    r = x - a.astype(f32)
    b = r.astype(bf16)
    return a, b, (r - b.astype(f32)).astype(bf16)


def lanes_of(x, j):
    return jnp.broadcast_to(x[:, j : j + 1], (8, BLOCK))


def row_of(x, i):
    return jnp.broadcast_to(x[i : i + 1, :], (8, BLOCK))


def invert_block(d_ref, half_way):
    lane = lax.broadcasted_iota(jnp.int32, (8, BLOCK), 1)
    sub = lax.broadcasted_iota(jnp.int32, (8, BLOCK), 0)
    groups = STRIP // 8
    for strip in range(BLOCK // STRIP):
        base = strip * STRIP
        rows = [d_ref[base + 8 * g : base + 8 * g + 8, :] for g in range(groups)]
        cols = [[lanes_of(rows[g], base + j) for g in range(groups)] for j in range(STRIP)]
        scale = [jnp.zeros((8, BLOCK), f32)] * groups
        for i in range(STRIP):
            h, q = i // 8, i % 8
            pivot = row_of(cols[i][h], q)
            inv_pivot = 1.0 / pivot
            scale[h] = jnp.where(sub == q, lax.rsqrt(pivot), scale[h])
            f = [None] * groups
            f[h] = jnp.where(sub > q, cols[i][h], 0.0) * inv_pivot
            for g in range(h + 1, groups):
                f[g] = cols[i][g] * inv_pivot
            for j in range(i + 1, STRIP):
                t = row_of(cols[j][h], q)
                for g in range(h, groups):
                    cols[j][g] = cols[j][g] - f[g] * t
            rows[h] = jnp.where(lane == base + i, jnp.where(sub == q, 1.0, 0.0), rows[h])
            for g in range(h + 1, groups):
                rows[g] = jnp.where(lane == base + i, 0.0, rows[g])
            t = row_of(rows[h], q)
            for g in range(h, groups):
                rows[g] = rows[g] - f[g] * t
        for g in range(groups):
            above = (lane > base + 8 * g + sub) & (lane < base + STRIP)
            rows[g] = jnp.where(above, 0.0, rows[g]) * scale[g]
            d_ref[base + 8 * g : base + 8 * g + 8, :] = rows[g]
        first = base + STRIP
        if strip == 3:
            half_way()
        if first < BLOCK:
            a, b, c = split3(jnp.concatenate(rows, axis=0))
            left = jnp.concatenate([a, a, b, a, b, c], axis=0)
            right = jnp.concatenate([a, b, a, c, b, a], axis=0)
            update = lax.dot_general(left, right, (((0,), (0,)), ((), ())), preferred_element_type=f32)
            wide = lax.broadcasted_iota(jnp.int32, (BLOCK - first, BLOCK), 1)
            old = jnp.where((wide >= base) & (wide < first), 0.0, d_ref[first:, :])
            d_ref[first:, :] = old - update[first:, :]


def hdot(a, b, dims):
    return lax.dot_general(a, b, (dims, ((), ())), precision=lax.Precision.HIGHEST, preferred_element_type=f32)


def fill_matrix(locs_ref, m_ref, n):
    blocks = n // BLOCK
    eye = lax.broadcasted_iota(jnp.int32, (BLOCK, BLOCK), 0) == lax.broadcasted_iota(jnp.int32, (BLOCK, BLOCK), 1)
    for bi in range(blocks):
        col = [jnp.transpose(jnp.broadcast_to(locs_ref[c : c + 1, bi * BLOCK : (bi + 1) * BLOCK], (BLOCK, BLOCK))) for c in (0, 1)]
        for bj in range(blocks):
            at = (slice(bi * BLOCK, (bi + 1) * BLOCK), slice(bj * BLOCK, (bj + 1) * BLOCK))
            if bj < bi:
                m_ref[at] = jnp.zeros((BLOCK, BLOCK), f32)
                continue
            row = [locs_ref[c : c + 1, bj * BLOCK : (bj + 1) * BLOCK] for c in (0, 1)]
            value = exp_distance(col[0] - row[0], col[1] - row[1])
            if bi == bj:
                value = value + jnp.where(eye, 0.1, 0.0)
            m_ref[at] = value


ROW_TILE = 256


def split2(x):
    high = x.astype(bf16)
    return high, (x - high.astype(f32)).astype(bf16)


def dot3(left, right):
    def one(a, b):
        return lax.dot_general(a, b, (((1,), (1,)), ((), ())), preferred_element_type=f32)

    return one(left[0], right[0]) + (one(left[0], right[1]) + one(left[1], right[0]))


def across(row):
    return jnp.transpose(jnp.broadcast_to(row, (BLOCK, BLOCK)))


def trailing_kernel(panel_ref, tile_ref, inv_ref, gap_ref, factor_ref, out_ref, factor_buf, out_buf, col_h, col_l, inv_h, inv_l, sems):
    rows = panel_ref.shape[1]
    inv_h[...], inv_l[...] = split2(inv_ref[...])
    col_h[...], col_l[...] = split2(dot3(split2(jnp.transpose(tile_ref[...])), (inv_h[...], inv_l[...])))

    def out_copy(buf, ref, which, i):
        at = pl.ds(i * ROW_TILE, ROW_TILE)
        return pltpu.make_async_copy(buf.at[at, :], ref.at[at, :], sems.at[which, i])

    for i in range(rows // ROW_TILE):
        at = slice(i * ROW_TILE, (i + 1) * ROW_TILE)
        factor = dot3(split2(jnp.transpose(panel_ref[:, at])), (inv_h[...], inv_l[...]))
        factor_buf[at, :] = factor
        out_copy(factor_buf, factor_ref, 0, i).start()
        update = dot3(split2(factor), (col_h[...], col_l[...]))
        out_buf[at, :] = gap_ref[at, :] - update
        out_copy(out_buf, out_ref, 1, i).start()
    for i in range(rows // ROW_TILE):
        out_copy(factor_buf, factor_ref, 0, i).wait()
        out_copy(out_buf, out_ref, 1, i).wait()


def trailing_update(panel_t, tile_t, inv_lower, gap):
    depth, rows = panel_t.shape
    width = gap.shape[1]
    vmem = pl.BlockSpec(memory_space=pltpu.VMEM)
    anywhere = pl.BlockSpec(memory_space=pl.ANY)
    return pl.pallas_call(
        trailing_kernel,
        out_shape=(jax.ShapeDtypeStruct((rows, depth), f32), jax.ShapeDtypeStruct((rows, width), f32)),
        in_specs=[vmem] * 4,
        out_specs=(anywhere, anywhere),
        scratch_shapes=[
            pltpu.VMEM((rows, depth), f32),
            pltpu.VMEM((rows, width), f32),
            pltpu.VMEM((width, depth), bf16),
            pltpu.VMEM((width, depth), bf16),
            pltpu.VMEM((depth, depth), bf16),
            pltpu.VMEM((depth, depth), bf16),
            pltpu.SemaphoreType.DMA((2, rows // ROW_TILE)),
        ],
        compiler_params=pltpu.CompilerParams(vmem_limit_bytes=VMEM_B),
        cost_estimate=pl.CostEstimate(flops=12 * rows * depth * width, bytes_accessed=16 * rows * width, transcendentals=0),
        name="trailing_update",
    )(panel_t, tile_t, inv_lower, gap)


MESH = pl.DeviceIdType.MESH


def invert_step(k, blocks, m_ref, d_ref, inv_ref, hand_over):
    n = m_ref.shape[1]
    lower = lax.broadcasted_iota(jnp.int32, (BLOCK, BLOCK), 0) >= lax.broadcasted_iota(jnp.int32, (BLOCK, BLOCK), 1)
    lane_block = lax.broadcasted_iota(jnp.int32, (BLOCK, n), 1) // BLOCK
    mine = pl.ds(pl.multiple_of(k * BLOCK, BLOCK), BLOCK)
    d_ref[...] = m_ref[mine, mine]
    invert_block(d_ref, lambda: hand_over(0))
    w = jnp.where(lower, d_ref[...], 0.0)
    m_ref[mine, :] = hdot(w, m_ref[mine, :], ((1,), (0,)))
    m_ref[mine, mine] = w
    row = m_ref[mine, :]
    inv_ref[mine, :] = jnp.where(lane_block <= k, row, 0.0)

    def below(i, carry):
        his = pl.ds(pl.multiple_of(i * BLOCK, BLOCK), BLOCK)
        update = hdot(m_ref[mine, his], row, ((0,), (0,)))
        m_ref[his, :] = jnp.where(lane_block == k, 0.0, m_ref[his, :]) - update
        return carry

    hand_over(1)
    lax.fori_loop(k + 1, blocks, below, 0)


TRAIL_PARTS = 4


def trail_copy(trail_ref, trail_buf, trail_sems, part):
    size = trail_buf.shape[0] // TRAIL_PARTS
    at = pl.ds(part * size, size)
    return pltpu.make_async_copy(trail_ref.at[at, :], trail_buf.at[at, :], trail_sems.at[part])


def fill_gap(b, same, row_locs_ref, col_locs_ref, trail_buf, gap_ref):
    rows = pl.ds(pl.multiple_of(b * BLOCK, BLOCK), BLOCK)
    width = gap_ref.shape[1]
    xr, yr = across(row_locs_ref[0:1, rows]), across(row_locs_ref[1:2, rows])
    i = lax.broadcasted_iota(jnp.int32, (BLOCK, BLOCK), 0) + b * BLOCK
    for block in range(width // BLOCK):
        cols = slice(block * BLOCK, (block + 1) * BLOCK)
        value = exp_distance(xr - col_locs_ref[0:1, cols], yr - col_locs_ref[1:2, cols])
        j = lax.broadcasted_iota(jnp.int32, (BLOCK, BLOCK), 1) + block * BLOCK
        value = value + jnp.where((i == j) & same, 0.1, 0.0)
        gap_ref[rows, cols] = value - trail_buf[rows, cols]


def gather_kernel(
    locs_hbm, row_locs_hbm, prior_hbm, trail_ref,
    panel_ref, tile_ref, inv_ref, gap_ref,
    m_ref, d_ref, part_ref, turn_ref, trail_buf, col_locs_ref, locs_ref, row_locs_ref, prior_ref, trail_sems, in_sems,
    slice_send, slice_recv, piece_send, piece_recv, block_send, block_recv, swap_send, locs_recv, own_sem,
):
    n = locs_ref.shape[1]
    width, rows = prior_ref.shape
    tile = col_locs_ref.shape[1]
    blocks = n // BLOCK
    row, col = lax.axis_index("row"), lax.axis_index("col")
    x, z_hi = lax.div(row, 4), lax.rem(row, 4)
    z_lo, y, core = lax.div(col, 8), lax.rem(lax.div(col, 2), 4), lax.rem(col, 2)

    def near(i):
        return [lax.rem(i + d, 4) for d in (3, 1, 2)]

    def col_of(a, b, c):
        return a * 8 + b * 2 + c

    sibling = col_of(z_lo, y, 1 - core)
    partner = col_of(1 - z_lo, y, core)
    y_own = [col_of(z_lo, b, core) for b in near(y)]
    y_far = [col_of(1 - z_lo, b, core) for b in near(y)]
    z_rows = [x * 4 + b for b in near(z_hi)]
    x_near = near(x)
    x_rows = [b * 4 + z_hi for b in x_near]

    loads = [
        pltpu.make_async_copy(src, dst, in_sems.at[i])
        for i, (src, dst) in enumerate([(locs_hbm, locs_ref), (row_locs_hbm, row_locs_ref), (prior_hbm, prior_ref)])
    ]
    for copy in loads:
        copy.start()
    barrier = pltpu.get_barrier_semaphore()
    for b in range(TRAIL_PARTS):
        trail_copy(trail_ref, trail_buf, trail_sems, b).start()
    for c in [sibling, partner] + y_own[:2]:
        pl.semaphore_signal(barrier, inc=1, device_id=(row, c), device_id_type=MESH)
    for r in z_rows[:2] + x_rows[:2]:
        pl.semaphore_signal(barrier, inc=1, device_id=(r, col), device_id_type=MESH)

    @pl.when(row != col)
    def _():
        pl.semaphore_signal(barrier, inc=1, device_id=(col, row), device_id_type=MESH)

    for copy in loads:
        copy.wait()

    at = pl.ds(pl.multiple_of(lax.div(col, 4) * BLOCK, BLOCK), BLOCK)
    mine = pl.ds(pl.multiple_of(lax.rem(col, 4) * width, width), width)
    for c in (0, 1):
        turn_ref[c] = across(locs_ref[c : c + 1, at])
    for b in range(rows // BLOCK):
        s = slice(b * BLOCK, (b + 1) * BLOCK)
        value = exp_distance(turn_ref[0, mine, :] - row_locs_ref[0:1, s], turn_ref[1, mine, :] - row_locs_ref[1:2, s])
        part_ref[:, s] = value - prior_ref[:, s]

    pl.semaphore_wait(barrier, jnp.where(row == col, 8, 9))

    def cut(ref, index, size, half):
        if half is None:
            return ref.at[pl.ds(pl.multiple_of(index * size, size), size), :]
        return ref.at[pl.ds(pl.multiple_of(index * size + half * (size // 2), size // 2), size // 2), :]

    def slice_of(c, half=None):
        return cut(panel_ref, c, width, half)

    def piece_of(r, half=None):
        return cut(tile_ref, r, width, half)

    def block_of(b, half=None):
        return cut(tile_ref, b, 4 * width, half)

    sent = []

    def send(of, sends, recvs, index, half, to, src=None):
        slot = sum(1 for entry in sent if entry[1] is sends)
        sent.append((of, sends, slot, half))
        dst = of(index, half)
        pltpu.make_async_remote_copy(
            src_ref=dst if src is None else src,
            dst_ref=dst,
            send_sem=sends.at[slot],
            recv_sem=recvs.at[index, half or 0],
            device_id=to,
            device_id_type=MESH,
        ).start()

    def send_slice(c, to_col, half=None, src=None):
        send(slice_of, slice_send, slice_recv, c, half, (row, to_col), src)

    def send_piece(r, to_row, half=None):
        send(piece_of, piece_send, piece_recv, r, half, (to_row, col))

    def send_block(b, to_row, half=None):
        send(block_of, block_send, block_recv, b, half, (to_row, col))

    def wait_bytes(ref, sem):
        pltpu.make_async_copy(ref, ref, sem).wait()

    def arrived(of, recvs, index, half=None):
        wait_bytes(of(index, half), recvs.at[index, half or 0])

    own_copy = pltpu.make_async_copy(part_ref, slice_of(col), own_sem)
    swap_src = part_ref.at[:, 0:tile]
    locs_src = row_locs_ref.at[:, 0:tile]
    swap_copy = pltpu.make_async_remote_copy(src_ref=swap_src, dst_ref=piece_of(col), send_sem=swap_send.at[0], recv_sem=piece_recv.at[col, 0], device_id=(col, row), device_id_type=MESH)
    locs_copy = pltpu.make_async_remote_copy(src_ref=locs_src, dst_ref=col_locs_ref, send_sem=swap_send.at[1], recv_sem=locs_recv, device_id=(col, row), device_id_type=MESH)

    @pl.when(row != col)
    def _():
        swap_copy.start()
        locs_copy.start()

    @pl.when(row == col)
    def _():
        pltpu.make_async_copy(swap_src, piece_of(row), piece_recv.at[row, 0]).start()
        pltpu.make_async_copy(locs_src, col_locs_ref, locs_recv).start()

    send_slice(col, partner, src=part_ref)
    for c in y_own[:2]:
        send_slice(col, c, src=part_ref)
    send_slice(col, sibling, src=part_ref)
    own_copy.start()

    def tile_to_z():
        arrived(piece_of, piece_recv, row)
        for r in z_rows[:2]:
            send_piece(row, r)

    def partner_to_y():
        arrived(slice_of, slice_recv, partner)
        for c in y_own[:2]:
            send_slice(partner, c)
        send_slice(partner, sibling)

    def pass_on(sources, targets):
        for h in (0, 1):
            arrived(slice_of, slice_recv, sources[h])
            send_slice(sources[h], targets[1 - h], half=h)
            send_slice(sources[h], sibling)

    def opposite_slice(c):
        for h in (0, 1):
            arrived(slice_of, slice_recv, c, h)
        send_slice(c, sibling)

    def pieces_on():
        for h in (0, 1):
            arrived(piece_of, piece_recv, z_rows[h])
            send_piece(z_rows[h], z_rows[1 - h], half=h)

    def tile_to_x():
        for h in (0, 1):
            arrived(piece_of, piece_recv, z_rows[2], h)
        for r in x_rows[:2]:
            send_block(x, r)

    def blocks_on():
        for h in (0, 1):
            arrived(block_of, block_recv, x_near[h])
            send_block(x_near[h], x_rows[1 - h], half=h)

    stages = {
        0: [tile_to_z],
        1: [partner_to_y, lambda: pass_on(y_own, y_own)],
        2: [pieces_on],
        3: [tile_to_x],
        4: [lambda: pass_on(y_far, y_own)],
        5: [lambda: opposite_slice(y_own[2])],
        6: [blocks_on, lambda: opposite_slice(y_far[2])],
    }

    late = {}

    fill_matrix(locs_ref, m_ref, n)

    def one_block(k, carry):
        def hand_over(part):
            for stage in range(part, 2 * blocks, 2):
                if stage in stages:
                    @pl.when(k == stage // 2)
                    def _():
                        for task in stages[stage]:
                            task()

        invert_step(k, blocks, m_ref, d_ref, inv_ref, hand_over)
        return carry

    lax.fori_loop(0, blocks, one_block, 0)

    wait_bytes(col_locs_ref, locs_recv)
    for part in range(TRAIL_PARTS):
        trail_copy(trail_ref, trail_buf, trail_sems, part).wait()

    def one_gap(b, carry):
        fill_gap(b, row == col, row_locs_ref, col_locs_ref, trail_buf, gap_ref)
        for step, tasks in late.items():
            @pl.when(b == step)
            def _():
                for task in tasks:
                    task()
        return carry

    lax.fori_loop(0, rows // BLOCK, one_gap, 0)

    for a in range(2):
        for b in range(4):
            arrived(slice_of, slice_recv, col_of(a, b, 1 - core))
    for h in (0, 1):
        arrived(block_of, block_recv, x_near[2], h)
    own_copy.wait()
    for of, sends, slot, half in sent:
        wait_bytes(of(0, half), sends.at[slot])

    @pl.when(row != col)
    def _():
        swap_copy.wait_send()
        locs_copy.wait_send()


def gather_and_invert(panel_locs, row_locs, prior_t, prior_trail):
    n = panel_locs.shape[1]
    width, rows = prior_t.shape
    n_col = n // width
    tile = prior_trail.shape[1]
    vmem = pl.BlockSpec(memory_space=pltpu.VMEM)
    anywhere = pl.BlockSpec(memory_space=pl.ANY)
    dma = pltpu.SemaphoreType.DMA
    return pl.pallas_call(
        gather_kernel,
        out_shape=(
            jax.ShapeDtypeStruct((n, rows), f32),
            jax.ShapeDtypeStruct((n, tile), f32),
            jax.ShapeDtypeStruct((n, n), f32),
            jax.ShapeDtypeStruct((rows, tile), f32),
        ),
        in_specs=[pl.BlockSpec(memory_space=pltpu.HBM)] * 4,
        out_specs=(vmem, vmem, vmem, vmem),
        scratch_shapes=[
            pltpu.VMEM((n, n), f32),
            pltpu.VMEM((BLOCK, BLOCK), f32),
            pltpu.VMEM((width, rows), f32),
            pltpu.VMEM((2, BLOCK, BLOCK), f32),
            pltpu.VMEM((rows, tile), f32),
            pltpu.VMEM((2, tile), f32),
            pltpu.VMEM((2, n), f32),
            pltpu.VMEM((2, rows), f32),
            pltpu.VMEM((width, rows), f32),
            dma((TRAIL_PARTS,)),
            dma((3,)),
            dma((17,)), dma((n_col, 2)), dma((4,)), dma((n_col, 2)), dma((4,)), dma((4, 2)), dma((2,)), dma, dma,
        ],
        compiler_params=pltpu.CompilerParams(vmem_limit_bytes=VMEM_A, collective_id=0, has_side_effects=True),
        cost_estimate=pl.CostEstimate(flops=2 * n**3, bytes_accessed=8 * n * n, transcendentals=n * n),
        name="gather_and_invert",
    )(panel_locs, row_locs, prior_t, prior_trail)


def body(row_locs, panel_locs, prior_panel, prior_trail):
    inputs = [pltpu.with_memory_space_constraint(a, pltpu.HBM) for a in (panel_locs, row_locs, prior_panel.T, prior_trail)]
    return trailing_update(*gather_and_invert(*inputs))


def solution(mesh):
    in_specs = (P(None, "row"), P(), P("row", "col"), P("row", "col"))
    out_specs = (P("row", None), P("row", "col"))
    return jax.shard_map(body, mesh=mesh, in_specs=in_specs, out_specs=out_specs, check_vma=False)
```

```python
import jax
import jax.numpy as jnp
from jax import lax
from jax.experimental import pallas as pl
from jax.experimental.pallas import tpu as pltpu
from jax.sharding import PartitionSpec as P

STRIP = 16
BLOCK = 128
VMEM_A = 24 * 2**20
VMEM_B = 24 * 2**20
f32, bf16 = jnp.float32, jnp.bfloat16


def exp_distance(dx, dy):
    d2 = dx * dx + dy * dy
    return jnp.exp(d2 * lax.rsqrt(jnp.maximum(d2, 1e-30)) * -10.0)


def split3(x):
    a = x.astype(bf16)
    r = x - a.astype(f32)
    b = r.astype(bf16)
    return a, b, (r - b.astype(f32)).astype(bf16)


def lanes_of(x, j):
    return jnp.broadcast_to(x[:, j : j + 1], (8, BLOCK))


def row_of(x, i):
    return jnp.broadcast_to(x[i : i + 1, :], (8, BLOCK))


def invert_block(d_ref, k, hand_over, beside):
    lane = lax.broadcasted_iota(jnp.int32, (8, BLOCK), 1)
    sub = lax.broadcasted_iota(jnp.int32, (8, BLOCK), 0)
    groups = STRIP // 8
    for strip in range(BLOCK // STRIP):
        base = strip * STRIP
        rows = [d_ref[base + 8 * g : base + 8 * g + 8, :] for g in range(groups)]
        cols = [[lanes_of(rows[g], base + j) for g in range(groups)] for j in range(STRIP)]
        scale = [jnp.zeros((8, BLOCK), f32)] * groups
        for i in range(STRIP):
            h, q = i // 8, i % 8
            pivot = row_of(cols[i][h], q)
            inv_pivot = 1.0 / pivot
            scale[h] = jnp.where(sub == q, lax.rsqrt(pivot), scale[h])
            f = [None] * groups
            f[h] = jnp.where(sub > q, cols[i][h], 0.0) * inv_pivot
            for g in range(h + 1, groups):
                f[g] = cols[i][g] * inv_pivot
            for j in range(i + 1, STRIP):
                t = row_of(cols[j][h], q)
                for g in range(h, groups):
                    cols[j][g] = cols[j][g] - f[g] * t
            rows[h] = jnp.where(lane == base + i, jnp.where(sub == q, 1.0, 0.0), rows[h])
            for g in range(h + 1, groups):
                rows[g] = jnp.where(lane == base + i, 0.0, rows[g])
            t = row_of(rows[h], q)
            for g in range(h, groups):
                rows[g] = rows[g] - f[g] * t
        for g in range(groups):
            above = (lane > base + 8 * g + sub) & (lane < base + STRIP)
            rows[g] = jnp.where(above, 0.0, rows[g]) * scale[g]
            d_ref[base + 8 * g : base + 8 * g + 8, :] = rows[g]
        first = base + STRIP
        if beside is not None and strip in BESIDE:
            beside(k, BESIDE.index(strip))
        if first < BLOCK:
            a, b, c = split3(jnp.concatenate(rows, axis=0))
            left = jnp.concatenate([a, a, b, a, b, c], axis=0)
            right = jnp.concatenate([a, b, a, c, b, a], axis=0)
            update = lax.dot_general(left, right, (((0,), (0,)), ((), ())), preferred_element_type=f32)
            wide = lax.broadcasted_iota(jnp.int32, (BLOCK - first, BLOCK), 1)
            old = jnp.where((wide >= base) & (wide < first), 0.0, d_ref[first:, :])
            d_ref[first:, :] = old - update[first:, :]
        if strip % 2:
            hand_over(k, strip // 2)


def hdot(a, b, dims):
    return lax.dot_general(a, b, (dims, ((), ())), precision=lax.Precision.HIGHEST, preferred_element_type=f32)


def fill_matrix(locs_ref, m_ref, n):
    blocks = n // BLOCK
    eye = lax.broadcasted_iota(jnp.int32, (BLOCK, BLOCK), 0) == lax.broadcasted_iota(jnp.int32, (BLOCK, BLOCK), 1)
    for bi in range(blocks):
        col = [jnp.transpose(jnp.broadcast_to(locs_ref[c : c + 1, bi * BLOCK : (bi + 1) * BLOCK], (BLOCK, BLOCK))) for c in (0, 1)]
        for bj in range(blocks):
            at = (slice(bi * BLOCK, (bi + 1) * BLOCK), slice(bj * BLOCK, (bj + 1) * BLOCK))
            if bj < bi:
                m_ref[at] = jnp.zeros((BLOCK, BLOCK), f32)
                continue
            row = [locs_ref[c : c + 1, bj * BLOCK : (bj + 1) * BLOCK] for c in (0, 1)]
            value = exp_distance(col[0] - row[0], col[1] - row[1])
            if bi == bj:
                value = value + jnp.where(eye, 0.1, 0.0)
            m_ref[at] = value


ROW_TILE = 256


def split2(x):
    high = x.astype(bf16)
    return high, (x - high.astype(f32)).astype(bf16)


def dot3(left, right):
    def one(a, b):
        return lax.dot_general(a, b, (((1,), (1,)), ((), ())), preferred_element_type=f32)

    return one(left[0], right[0]) + (one(left[0], right[1]) + one(left[1], right[0]))


def across(row):
    return jnp.transpose(jnp.broadcast_to(row, (BLOCK, BLOCK)))


def trailing_kernel(panel_ref, tile_ref, inv_ref, gap_ref, factor_ref, out_ref, factor_buf, out_buf, tile_buf, col_h, col_l, inv_h, inv_l, sems):
    rows = panel_ref.shape[1]
    inv_h[...], inv_l[...] = split2(inv_ref[...])
    col = lax.axis_index("col")
    piece = tile_ref.shape[0] // 16
    for r in range(16):
        at = pl.ds(pl.multiple_of(piece_column(r, col) * piece, piece), piece)
        tile_buf[at, :] = tile_ref[r * piece : (r + 1) * piece, :]
    col_h[...], col_l[...] = split2(dot3(split2(jnp.transpose(tile_buf[...])), (inv_h[...], inv_l[...])))

    def out_copy(buf, ref, which, i):
        at = pl.ds(i * ROW_TILE, ROW_TILE)
        return pltpu.make_async_copy(buf.at[at, :], ref.at[at, :], sems.at[which, i])

    for i in range(rows // ROW_TILE):
        at = slice(i * ROW_TILE, (i + 1) * ROW_TILE)
        factor = dot3(split2(jnp.transpose(panel_ref[:, at])), (inv_h[...], inv_l[...]))
        factor_buf[at, :] = factor
        out_copy(factor_buf, factor_ref, 0, i).start()
        update = dot3(split2(factor), (col_h[...], col_l[...]))
        out_buf[at, :] = gap_ref[at, :] - update
        out_copy(out_buf, out_ref, 1, i).start()
    for i in range(rows // ROW_TILE):
        out_copy(factor_buf, factor_ref, 0, i).wait()
        out_copy(out_buf, out_ref, 1, i).wait()


def trailing_update(panel_t, tile_t, inv_lower, gap):
    depth, rows = panel_t.shape
    width = gap.shape[1]
    vmem = pl.BlockSpec(memory_space=pltpu.VMEM)
    anywhere = pl.BlockSpec(memory_space=pl.ANY)
    return pl.pallas_call(
        trailing_kernel,
        out_shape=(jax.ShapeDtypeStruct((rows, depth), f32), jax.ShapeDtypeStruct((rows, width), f32)),
        in_specs=[vmem] * 4,
        out_specs=(anywhere, anywhere),
        scratch_shapes=[
            pltpu.VMEM((rows, depth), f32),
            pltpu.VMEM((rows, width), f32),
            pltpu.VMEM((depth, width), f32),
            pltpu.VMEM((width, depth), bf16),
            pltpu.VMEM((width, depth), bf16),
            pltpu.VMEM((depth, depth), bf16),
            pltpu.VMEM((depth, depth), bf16),
            pltpu.SemaphoreType.DMA((2, rows // ROW_TILE)),
        ],
        compiler_params=pltpu.CompilerParams(vmem_limit_bytes=VMEM_B),
        cost_estimate=pl.CostEstimate(flops=12 * rows * depth * width, bytes_accessed=16 * rows * width, transcendentals=0),
        name="trailing_update",
    )(panel_t, tile_t, inv_lower, gap)


MESH = pl.DeviceIdType.MESH


def invert_step(k, blocks, m_ref, d_ref, inv_ref, hand_over, beside):
    n = m_ref.shape[1]
    lower = lax.broadcasted_iota(jnp.int32, (BLOCK, BLOCK), 0) >= lax.broadcasted_iota(jnp.int32, (BLOCK, BLOCK), 1)
    lane_block = lax.broadcasted_iota(jnp.int32, (BLOCK, n), 1) // BLOCK
    mine = pl.ds(pl.multiple_of(k * BLOCK, BLOCK), BLOCK)
    d_ref[...] = m_ref[mine, mine]
    invert_block(d_ref, k, hand_over, beside)
    w = jnp.where(lower, d_ref[...], 0.0)
    m_ref[mine, :] = hdot(w, m_ref[mine, :], ((1,), (0,)))
    m_ref[mine, mine] = w
    row = m_ref[mine, :]
    inv_ref[mine, :] = jnp.where(lane_block <= k, row, 0.0)

    def below(i, carry):
        his = pl.ds(pl.multiple_of(i * BLOCK, BLOCK), BLOCK)
        update = hdot(m_ref[mine, his], row, ((0,), (0,)))
        m_ref[his, :] = jnp.where(lane_block == k, 0.0, m_ref[his, :]) - update
        return carry

    lax.fori_loop(k + 1, blocks, below, 0)


TRAIL_PARTS = 4
POINTS = 4
BESIDE = (0, 1, 3, 4, 6, 7)


def trail_copy(trail_ref, trail_buf, trail_sems, part):
    size = trail_buf.shape[0] // TRAIL_PARTS
    at = pl.ds(part * size, size)
    return pltpu.make_async_copy(trail_ref.at[at, :], trail_buf.at[at, :], trail_sems.at[part])


def fill_gap(b, same, row_locs_ref, col_locs_ref, trail_buf, gap_ref):
    rows = pl.ds(pl.multiple_of(b * BLOCK, BLOCK), BLOCK)
    width = gap_ref.shape[1]
    xr, yr = across(row_locs_ref[0:1, rows]), across(row_locs_ref[1:2, rows])
    i = lax.broadcasted_iota(jnp.int32, (BLOCK, BLOCK), 0) + b * BLOCK
    for block in range(width // BLOCK):
        cols = slice(block * BLOCK, (block + 1) * BLOCK)
        value = exp_distance(xr - col_locs_ref[0:1, cols], yr - col_locs_ref[1:2, cols])
        j = lax.broadcasted_iota(jnp.int32, (BLOCK, BLOCK), 1) + block * BLOCK
        value = value + jnp.where((i == j) & same, 0.1, 0.0)
        gap_ref[rows, cols] = value - trail_buf[rows, cols]


def piece_column(row, col):
    turn = lax.rem(row + 16 - col, 16)
    return lax.rem(turn, 2) * 8 + lax.div(turn, 4) * 2 + lax.rem(lax.div(turn, 2), 2)


def gather_kernel(
    locs_hbm, row_locs_hbm, prior_hbm, trail_ref,
    panel_ref, tile_ref, inv_ref, gap_ref,
    m_ref, d_ref, part_ref, turn_ref, trail_buf, col_locs_ref, locs_ref, row_locs_ref, prior_ref, trail_sems, in_sems,
    slice_send, slice_recv, piece_send, piece_recv, pair_send, pair_recv, swap_send, locs_recv, own_sem,
):
    n = locs_ref.shape[1]
    width, rows = prior_ref.shape
    tile = col_locs_ref.shape[1]
    blocks = n // BLOCK
    row, col = lax.axis_index("row"), lax.axis_index("col")
    x, z_hi = lax.div(row, 4), lax.rem(row, 4)
    z_lo, y, core = lax.div(col, 8), lax.rem(lax.div(col, 2), 4), lax.rem(col, 2)

    def near(i):
        return [lax.rem(i + d, 4) for d in (3, 1, 2)]

    def col_of(a, b, c):
        return a * 8 + b * 2 + c

    sibling = col_of(z_lo, y, 1 - core)
    partner = col_of(1 - z_lo, y, core)
    y_own = [col_of(z_lo, b, core) for b in near(y)]
    y_far = [col_of(1 - z_lo, b, core) for b in near(y)]
    z_rows = [x * 4 + b for b in near(z_hi)]
    x_near = near(x)
    x_rows = [b * 4 + z_hi for b in x_near]

    swap_to = (lax.rem(y * 4 + core * 2 + z_lo + row, 16), row)
    swap_from = (col, piece_column(row, col))
    alone = row + col == 0

    loads = [
        pltpu.make_async_copy(src, dst, in_sems.at[i])
        for i, (src, dst) in enumerate([(locs_hbm, locs_ref), (row_locs_hbm, row_locs_ref), (prior_hbm, prior_ref)])
    ]
    for copy in loads:
        copy.start()
    barrier = pltpu.get_barrier_semaphore()
    for b in range(TRAIL_PARTS):
        trail_copy(trail_ref, trail_buf, trail_sems, b).start()
    for c in [sibling, partner] + y_own[:2]:
        pl.semaphore_signal(barrier, inc=1, device_id=(row, c), device_id_type=MESH)
    for r in z_rows[:2] + x_rows[:2]:
        pl.semaphore_signal(barrier, inc=1, device_id=(r, col), device_id_type=MESH)

    @pl.when(jnp.logical_not(alone))
    def _():
        pl.semaphore_signal(barrier, inc=1, device_id=swap_from, device_id_type=MESH)

    for copy in loads:
        copy.wait()

    at = pl.ds(pl.multiple_of(lax.div(col, 4) * BLOCK, BLOCK), BLOCK)
    mine = pl.ds(pl.multiple_of(lax.rem(col, 4) * width, width), width)
    for c in (0, 1):
        turn_ref[c] = across(locs_ref[c : c + 1, at])
    def fill_part(first, last):
        for b in range(first // BLOCK, last // BLOCK):
            s = slice(b * BLOCK, (b + 1) * BLOCK)
            value = exp_distance(turn_ref[0, mine, :] - row_locs_ref[0:1, s], turn_ref[1, mine, :] - row_locs_ref[1:2, s])
            part_ref[:, s] = value - prior_ref[:, s]

    fill_part(0, tile)
    pl.semaphore_wait(barrier, jnp.where(alone, 8, 9))

    def cut(ref, index, size, half):
        if half is None:
            return ref.at[pl.ds(pl.multiple_of(index * size, size), size), :]
        return ref.at[pl.ds(pl.multiple_of(index * size + half * (size // 2), size // 2), size // 2), :]

    def slice_of(c, half=None):
        return cut(panel_ref, c, width, half)

    def piece_of(r, half=None):
        return cut(tile_ref, r, width, half)

    sent = []

    def send(of, sends, recvs, index, half, to, src=None):
        slot = sum(1 for entry in sent if entry[1] is sends)
        sent.append((of, sends, slot, half))
        dst = of(index, half)
        pltpu.make_async_remote_copy(
            src_ref=dst if src is None else src,
            dst_ref=dst,
            send_sem=sends.at[slot],
            recv_sem=recvs.at[index, half or 0],
            device_id=to,
            device_id_type=MESH,
        ).start()

    def send_slice(c, to_col, half=None, src=None):
        send(slice_of, slice_send, slice_recv, c, half, (row, to_col), src)

    def send_piece(r, to_row, half=None):
        send(piece_of, piece_send, piece_recv, r, half, (to_row, col))

    def wait_bytes(ref, sem):
        pltpu.make_async_copy(ref, ref, sem).wait()

    def arrived(of, recvs, index, half=None):
        wait_bytes(of(index, half), recvs.at[index, half or 0])

    own_copy = pltpu.make_async_copy(part_ref, slice_of(col), own_sem)
    swap_src = part_ref.at[:, 0:tile]
    locs_src = row_locs_ref.at[:, 0:tile]
    swap_copy = pltpu.make_async_remote_copy(src_ref=swap_src, dst_ref=piece_of(swap_to[0]), send_sem=swap_send.at[0], recv_sem=piece_recv.at[swap_to[0], 0], device_id=swap_to, device_id_type=MESH)
    locs_copy = pltpu.make_async_remote_copy(src_ref=locs_src, dst_ref=col_locs_ref, send_sem=swap_send.at[1], recv_sem=locs_recv, device_id=swap_to, device_id_type=MESH)

    @pl.when(jnp.logical_not(alone))
    def _():
        swap_copy.start()
        locs_copy.start()

    @pl.when(alone)
    def _():
        pltpu.make_async_copy(swap_src, piece_of(row), piece_recv.at[row, 0]).start()
        pltpu.make_async_copy(locs_src, col_locs_ref, locs_recv).start()

    fill_part(tile, rows)
    send_slice(col, partner, src=part_ref)
    half_rows = [part_ref.at[pl.ds(h * (width // 2), width // 2), :] for h in (0, 1)]
    for h in (0, 1):
        send_slice(col, y_own[1], half=h, src=half_rows[h])
        send_slice(col, y_own[0], half=1 - h, src=half_rows[1 - h])
    send_slice(col, sibling, src=part_ref)
    own_copy.start()

    def tile_on():
        arrived(piece_of, piece_recv, row)
        for r in z_rows[:2] + x_rows[:2]:
            send_piece(row, r)

    def partner_to_y():
        arrived(slice_of, slice_recv, partner)
        for h in (0, 1):
            send_slice(partner, y_own[1], half=h)
            send_slice(partner, y_own[0], half=1 - h)
        send_slice(partner, sibling)

    def pass_on(sources):
        for h in (0, 1):
            arrived(slice_of, slice_recv, sources[h], h)
            send_slice(sources[h], y_own[1 - h], half=h)

    def to_sibling(sources):
        for h in (0, 1):
            arrived(slice_of, slice_recv, sources[h], 1 - h)
            send_slice(sources[h], sibling)

    def opposite_slice(c):
        for h in (0, 1):
            arrived(slice_of, slice_recv, c, h)
        send_slice(c, sibling)

    def pieces_on():
        for h in (0, 1):
            arrived(piece_of, piece_recv, z_rows[h])
            send_piece(z_rows[h], z_rows[1 - h], half=h)
            for r in x_rows[:2]:
                send_piece(z_rows[h], r)

    def opposite_piece():
        for h in (0, 1):
            arrived(piece_of, piece_recv, z_rows[2], h)
        for r in x_rows[:2]:
            send_piece(z_rows[2], r)

    def pair_of(b, half):
        return cut(tile_ref, b, 4 * width, half)

    def tiles_on():
        for h in (0, 1):
            for e in range(4):
                arrived(piece_of, piece_recv, x_near[h] * 4 + e)
            send(pair_of, pair_send, pair_recv, x_near[h], h, (x_rows[1 - h], col))

    schedule = [(2, "own"), (3, "tile_on"), (4, "partner_to_y"), (4, "own_over"), (7, "pieces_on"), (7, "opposite_own"), (9, "opposite_piece"), (9, "far"), (11, "far_over"), (11, "tiles_on"), (13, "opposite_far")]
    tasks = dict(
        tile_on=tile_on,
        partner_to_y=partner_to_y,
        own=lambda: pass_on(y_own),
        own_over=lambda: to_sibling(y_own),
        far=lambda: pass_on(y_far),
        far_over=lambda: to_sibling(y_far),
        opposite_own=lambda: opposite_slice(y_own[2]),
        opposite_far=lambda: opposite_slice(y_far[2]),
        pieces_on=pieces_on,
        opposite_piece=opposite_piece,
        tiles_on=tiles_on,
    )
    stages = {}
    for stage, name in schedule:
        stages.setdefault(stage, []).append(tasks[name])

    fill_matrix(locs_ref, m_ref, n)

    def hand_over(first, last):
        def at_strip(k, part):
            for stage in range(first * POINTS + part, last * POINTS, POINTS):
                if stage in stages:
                    @pl.when(k == stage // POINTS)
                    def _():
                        for task in stages[stage]:
                            task()

        return at_strip

    def beside(k, place):
        b = jnp.minimum((k - 1) * len(BESIDE) + place, rows // BLOCK - 1)
        fill_gap(b, row == col, row_locs_ref, col_locs_ref, trail_buf, gap_ref)

    invert_step(0, blocks, m_ref, d_ref, inv_ref, hand_over(0, 1), None)
    wait_bytes(col_locs_ref, locs_recv)
    for part in range(TRAIL_PARTS):
        trail_copy(trail_ref, trail_buf, trail_sems, part).wait()

    def one_block(k, carry):
        invert_step(k, blocks, m_ref, d_ref, inv_ref, hand_over(1, blocks), beside)
        return carry

    lax.fori_loop(1, blocks, one_block, 0)
    for stage in sorted(stages):
        if stage >= POINTS * blocks:
            for task in stages[stage]:
                task()

    for a in range(2):
        for b in range(4):
            arrived(slice_of, slice_recv, col_of(a, b, 1 - core))
    for h in (0, 1):
        wait_bytes(pair_of(x_near[2], h), pair_recv.at[x_near[2], h])
    own_copy.wait()
    for of, sends, slot, half in sent:
        wait_bytes(of(0, half), sends.at[slot])

    @pl.when(jnp.logical_not(alone))
    def _():
        swap_copy.wait_send()
        locs_copy.wait_send()


def gather_and_invert(panel_locs, row_locs, prior_t, prior_trail):
    n = panel_locs.shape[1]
    width, rows = prior_t.shape
    n_col = n // width
    tile = prior_trail.shape[1]
    vmem = pl.BlockSpec(memory_space=pltpu.VMEM)
    anywhere = pl.BlockSpec(memory_space=pl.ANY)
    dma = pltpu.SemaphoreType.DMA
    return pl.pallas_call(
        gather_kernel,
        out_shape=(
            jax.ShapeDtypeStruct((n, rows), f32),
            jax.ShapeDtypeStruct((n, tile), f32),
            jax.ShapeDtypeStruct((n, n), f32),
            jax.ShapeDtypeStruct((rows, tile), f32),
        ),
        in_specs=[pl.BlockSpec(memory_space=pltpu.HBM)] * 4,
        out_specs=(vmem, vmem, vmem, vmem),
        scratch_shapes=[
            pltpu.VMEM((n, n), f32),
            pltpu.VMEM((BLOCK, BLOCK), f32),
            pltpu.VMEM((width, rows), f32),
            pltpu.VMEM((2, BLOCK, BLOCK), f32),
            pltpu.VMEM((rows, tile), f32),
            pltpu.VMEM((2, tile), f32),
            pltpu.VMEM((2, n), f32),
            pltpu.VMEM((2, rows), f32),
            pltpu.VMEM((width, rows), f32),
            dma((TRAIL_PARTS,)),
            dma((3,)),
            dma((21,)), dma((n_col, 2)), dma((12,)), dma((n_col, 2)), dma((2,)), dma((4, 2)), dma((2,)), dma, dma,
        ],
        compiler_params=pltpu.CompilerParams(vmem_limit_bytes=VMEM_A, collective_id=0, has_side_effects=True),
        cost_estimate=pl.CostEstimate(flops=2 * n**3, bytes_accessed=8 * n * n, transcendentals=n * n),
        name="gather_and_invert",
    )(panel_locs, row_locs, prior_t, prior_trail)


def body(row_locs, panel_locs, prior_panel, prior_trail):
    inputs = [pltpu.with_memory_space_constraint(a, pltpu.HBM) for a in (panel_locs, row_locs, prior_panel.T, prior_trail)]
    return trailing_update(*gather_and_invert(*inputs))


def solution(mesh):
    in_specs = (P(None, "row"), P(), P("row", "col"), P("row", "col"))
    out_specs = (P("row", None), P("row", "col"))
    return jax.shard_map(body, mesh=mesh, in_specs=in_specs, out_specs=out_specs, check_vma=False)
```

```python
import jax
import jax.numpy as jnp
from jax import lax
from jax.experimental import pallas as pl
from jax.experimental.pallas import tpu as pltpu
from jax.sharding import PartitionSpec as P

STRIP = 16
AHEAD = 2
HAND_OVER = 2
BLOCK = 128
VMEM_A = 24 * 2**20
VMEM_B = 24 * 2**20
f32, bf16 = jnp.float32, jnp.bfloat16


def exp_distance(dx, dy):
    d2 = dx * dx + dy * dy
    return jnp.exp(d2 * lax.rsqrt(jnp.maximum(d2, 1e-30)) * -10.0)


def split3(x):
    a = x.astype(bf16)
    r = x - a.astype(f32)
    b = r.astype(bf16)
    return a, b, (r - b.astype(f32)).astype(bf16)


def lanes_of(x, j):
    return jnp.broadcast_to(x[:, j : j + 1], (8, BLOCK))


def row_of(x, i):
    return jnp.broadcast_to(x[i : i + 1, :], (8, BLOCK))


def invert_block(d_ref, k, hand_over, beside):
    lane = lax.broadcasted_iota(jnp.int32, (8, BLOCK), 1)
    sub = lax.broadcasted_iota(jnp.int32, (8, BLOCK), 0)
    own = STRIP // 8
    for strip in range(BLOCK // STRIP):
        base = strip * STRIP
        groups = min(own + AHEAD, (BLOCK - base) // 8)
        rows = [d_ref[base + 8 * g : base + 8 * g + 8, :] for g in range(groups)]
        cols = [[lanes_of(rows[g], base + j) for g in range(groups)] for j in range(STRIP)]
        scale = [jnp.zeros((8, BLOCK), f32)] * own
        for i in range(STRIP):
            h, q = i // 8, i % 8
            pivot = row_of(cols[i][h], q)
            inv_pivot = 1.0 / pivot
            scale[h] = jnp.where(sub == q, lax.rsqrt(pivot), scale[h])
            f = [None] * groups
            f[h] = jnp.where(sub > q, cols[i][h], 0.0) * inv_pivot
            for g in range(h + 1, groups):
                f[g] = cols[i][g] * inv_pivot
            for j in range(i + 1, STRIP):
                t = row_of(cols[j][h], q)
                for g in range(h, groups):
                    cols[j][g] = cols[j][g] - f[g] * t
            rows[h] = jnp.where(lane == base + i, jnp.where(sub == q, 1.0, 0.0), rows[h])
            for g in range(h + 1, groups):
                rows[g] = jnp.where(lane == base + i, 0.0, rows[g])
            t = row_of(rows[h], q)
            for g in range(h, groups):
                rows[g] = rows[g] - f[g] * t
        for g in range(own):
            above = (lane > base + 8 * g + sub) & (lane < base + STRIP)
            rows[g] = jnp.where(above, 0.0, rows[g]) * scale[g]
        for g in range(groups):
            d_ref[base + 8 * g : base + 8 * g + 8, :] = rows[g]
        if beside is not None and strip in BESIDE:
            beside(k, BESIDE.index(strip))
        first = base + 8 * groups
        if first < BLOCK:
            a, b, c = split3(jnp.concatenate(rows[:own], axis=0))
            left = jnp.concatenate([a, a, b, a, b, c], axis=0)
            right = jnp.concatenate([a, b, a, c, b, a], axis=0)
            update = lax.dot_general(left, right, (((0,), (0,)), ((), ())), preferred_element_type=f32)
            wide = lax.broadcasted_iota(jnp.int32, (BLOCK - first, BLOCK), 1)
            old = jnp.where((wide >= base) & (wide < base + STRIP), 0.0, d_ref[first:, :])
            d_ref[first:, :] = old - update[first:, :]
        if strip % HAND_OVER == HAND_OVER - 1:
            hand_over(k, strip // HAND_OVER)


def hdot(a, b, dims):
    return lax.dot_general(a, b, (dims, ((), ())), precision=lax.Precision.HIGHEST, preferred_element_type=f32)


def fill_matrix(locs_ref, m_ref, n, bi):
    blocks = n // BLOCK
    eye = lax.broadcasted_iota(jnp.int32, (BLOCK, BLOCK), 0) == lax.broadcasted_iota(jnp.int32, (BLOCK, BLOCK), 1)
    col = [jnp.transpose(jnp.broadcast_to(locs_ref[c : c + 1, bi * BLOCK : (bi + 1) * BLOCK], (BLOCK, BLOCK))) for c in (0, 1)]
    for bj in range(blocks):
        at = (slice(bi * BLOCK, (bi + 1) * BLOCK), slice(bj * BLOCK, (bj + 1) * BLOCK))
        if bj < bi:
            m_ref[at] = jnp.zeros((BLOCK, BLOCK), f32)
            continue
        row = [locs_ref[c : c + 1, bj * BLOCK : (bj + 1) * BLOCK] for c in (0, 1)]
        value = exp_distance(col[0] - row[0], col[1] - row[1])
        if bi == bj:
            value = value + jnp.where(eye, 0.1, 0.0)
        m_ref[at] = value


ROW_TILE = 256


def split2(x):
    high = x.astype(bf16)
    return high, (x - high.astype(f32)).astype(bf16)


def dot3(left, right):
    def one(a, b):
        return lax.dot_general(a, b, (((1,), (1,)), ((), ())), preferred_element_type=f32)

    return one(left[0], right[0]) + (one(left[0], right[1]) + one(left[1], right[0]))


def across(row):
    return jnp.transpose(jnp.broadcast_to(row, (BLOCK, BLOCK)))


def times_lower(left, inv_h, inv_l):
    half = inv_h.shape[0] // 2
    high, low = split2(left)
    top = dot3((high[:, :half], low[:, :half]), (inv_h[:half, :half], inv_l[:half, :half]))
    bottom = dot3((high, low), (inv_h[half:, :], inv_l[half:, :]))
    return jnp.concatenate([top, bottom], axis=1)


def trailing_kernel(panel_ref, tile_ref, inv_ref, gap_ref, factor_ref, out_ref, factor_buf, out_buf, tile_buf, col_h, col_l, inv_h, inv_l, sems):
    rows = panel_ref.shape[1]
    inv_h[...], inv_l[...] = split2(inv_ref[...])
    col = lax.axis_index("col")
    piece = tile_ref.shape[0] // 16
    for r in range(16):
        at = pl.ds(pl.multiple_of(piece_column(r, col) * piece, piece), piece)
        tile_buf[at, :] = tile_ref[r * piece : (r + 1) * piece, :]
    col_h[...], col_l[...] = split2(times_lower(jnp.transpose(tile_buf[...]), inv_h, inv_l))

    def out_copy(buf, ref, which, i):
        at = pl.ds(i * ROW_TILE, ROW_TILE)
        return pltpu.make_async_copy(buf.at[at, :], ref.at[at, :], sems.at[which, i])

    for i in range(rows // ROW_TILE):
        at = slice(i * ROW_TILE, (i + 1) * ROW_TILE)
        factor = times_lower(jnp.transpose(panel_ref[:, at]), inv_h, inv_l)
        factor_buf[at, :] = factor
        out_copy(factor_buf, factor_ref, 0, i).start()
        update = dot3(split2(factor), (col_h[...], col_l[...]))
        out_buf[at, :] = gap_ref[at, :] - update
        out_copy(out_buf, out_ref, 1, i).start()
    for i in range(rows // ROW_TILE):
        out_copy(factor_buf, factor_ref, 0, i).wait()
        out_copy(out_buf, out_ref, 1, i).wait()


def trailing_update(panel_t, tile_t, inv_lower, gap):
    depth, rows = panel_t.shape
    width = gap.shape[1]
    vmem = pl.BlockSpec(memory_space=pltpu.VMEM)
    anywhere = pl.BlockSpec(memory_space=pl.ANY)
    return pl.pallas_call(
        trailing_kernel,
        out_shape=(jax.ShapeDtypeStruct((rows, depth), f32), jax.ShapeDtypeStruct((rows, width), f32)),
        in_specs=[vmem] * 4,
        out_specs=(anywhere, anywhere),
        scratch_shapes=[
            pltpu.VMEM((rows, depth), f32),
            pltpu.VMEM((rows, width), f32),
            pltpu.VMEM((depth, width), f32),
            pltpu.VMEM((width, depth), bf16),
            pltpu.VMEM((width, depth), bf16),
            pltpu.VMEM((depth, depth), bf16),
            pltpu.VMEM((depth, depth), bf16),
            pltpu.SemaphoreType.DMA((2, rows // ROW_TILE)),
        ],
        compiler_params=pltpu.CompilerParams(vmem_limit_bytes=VMEM_B),
        cost_estimate=pl.CostEstimate(flops=12 * rows * depth * width, bytes_accessed=16 * rows * width, transcendentals=0),
        name="trailing_update",
    )(panel_t, tile_t, inv_lower, gap)


MESH = pl.DeviceIdType.MESH


def invert_step(k, blocks, m_ref, d_ref, inv_ref, hand_over, beside):
    n = m_ref.shape[1]
    lower = lax.broadcasted_iota(jnp.int32, (BLOCK, BLOCK), 0) >= lax.broadcasted_iota(jnp.int32, (BLOCK, BLOCK), 1)
    lane_block = lax.broadcasted_iota(jnp.int32, (BLOCK, n), 1) // BLOCK
    mine = pl.ds(pl.multiple_of(k * BLOCK, BLOCK), BLOCK)
    d_ref[...] = m_ref[mine, mine]
    invert_block(d_ref, k, hand_over, beside)
    w = jnp.where(lower, d_ref[...], 0.0)
    m_ref[mine, :] = hdot(w, m_ref[mine, :], ((1,), (0,)))
    m_ref[mine, mine] = w
    row = m_ref[mine, :]
    inv_ref[mine, :] = jnp.where(lane_block <= k, row, 0.0)

    def below(i, carry):
        his = pl.ds(pl.multiple_of(i * BLOCK, BLOCK), BLOCK)
        update = hdot(m_ref[mine, his], row, ((0,), (0,)))
        m_ref[his, :] = jnp.where(lane_block == k, 0.0, m_ref[his, :]) - update
        return carry

    lax.fori_loop(k + 1, blocks, below, 0)


TRAIL_PARTS = 4
POINTS = BLOCK // STRIP // HAND_OVER
BESIDE = (0, 1, 3, 4, 6, 7)


def trail_copy(trail_ref, trail_buf, trail_sems, part):
    size = trail_buf.shape[0] // TRAIL_PARTS
    at = pl.ds(part * size, size)
    return pltpu.make_async_copy(trail_ref.at[at, :], trail_buf.at[at, :], trail_sems.at[part])


def fill_gap(b, same, row_locs_ref, col_locs_ref, trail_buf, gap_ref):
    rows = pl.ds(pl.multiple_of(b * BLOCK, BLOCK), BLOCK)
    width = gap_ref.shape[1]
    xr, yr = across(row_locs_ref[0:1, rows]), across(row_locs_ref[1:2, rows])
    i = lax.broadcasted_iota(jnp.int32, (BLOCK, BLOCK), 0) + b * BLOCK
    for block in range(width // BLOCK):
        cols = slice(block * BLOCK, (block + 1) * BLOCK)
        value = exp_distance(xr - col_locs_ref[0:1, cols], yr - col_locs_ref[1:2, cols])
        j = lax.broadcasted_iota(jnp.int32, (BLOCK, BLOCK), 1) + block * BLOCK
        value = value + jnp.where((i == j) & same, 0.1, 0.0)
        gap_ref[rows, cols] = value - trail_buf[rows, cols]


def piece_column(row, col):
    turn = lax.rem(row + 16 - col, 16)
    return lax.rem(turn, 2) * 8 + lax.div(turn, 4) * 2 + lax.rem(lax.div(turn, 2), 2)


def gather_kernel(
    locs_hbm, row_locs_hbm, prior_hbm, trail_ref,
    panel_ref, tile_ref, inv_ref, gap_ref,
    m_ref, d_ref, part_ref, turn_ref, trail_buf, col_locs_ref, locs_ref, row_locs_ref, prior_ref, trail_sems, in_sems,
    slice_send, slice_recv, piece_send, piece_recv, pair_send, pair_recv, swap_send, locs_recv, own_sem,
):
    n = locs_ref.shape[1]
    width, rows = prior_ref.shape
    tile = col_locs_ref.shape[1]
    blocks = n // BLOCK
    row, col = lax.axis_index("row"), lax.axis_index("col")
    x, z_hi = lax.div(row, 4), lax.rem(row, 4)
    z_lo, y, core = lax.div(col, 8), lax.rem(lax.div(col, 2), 4), lax.rem(col, 2)

    def near(i):
        return [lax.rem(i + d, 4) for d in (3, 1, 2)]

    def col_of(a, b, c):
        return a * 8 + b * 2 + c

    sibling = col_of(z_lo, y, 1 - core)
    partner = col_of(1 - z_lo, y, core)
    y_own = [col_of(z_lo, b, core) for b in near(y)]
    y_far = [col_of(1 - z_lo, b, core) for b in near(y)]
    z_rows = [x * 4 + b for b in near(z_hi)]
    x_near = near(x)
    x_rows = [b * 4 + z_hi for b in x_near]

    swap_to = (lax.rem(y * 4 + core * 2 + z_lo + row, 16), row)
    swap_from = (col, piece_column(row, col))
    alone = row + col == 0

    loads = [
        pltpu.make_async_copy(src, dst, in_sems.at[i])
        for i, (src, dst) in enumerate([(locs_hbm, locs_ref), (row_locs_hbm, row_locs_ref), (prior_hbm, prior_ref)])
    ]
    for copy in loads:
        copy.start()
    barrier = pltpu.get_barrier_semaphore()
    for b in range(TRAIL_PARTS):
        trail_copy(trail_ref, trail_buf, trail_sems, b).start()
    for c in [sibling, partner] + y_own[:2]:
        pl.semaphore_signal(barrier, inc=1, device_id=(row, c), device_id_type=MESH)
    for r in z_rows[:2] + x_rows[:2]:
        pl.semaphore_signal(barrier, inc=1, device_id=(r, col), device_id_type=MESH)

    @pl.when(jnp.logical_not(alone))
    def _():
        pl.semaphore_signal(barrier, inc=1, device_id=swap_from, device_id_type=MESH)

    for copy in loads:
        copy.wait()

    at = pl.ds(pl.multiple_of(lax.div(col, 4) * BLOCK, BLOCK), BLOCK)
    mine = pl.ds(pl.multiple_of(lax.rem(col, 4) * width, width), width)
    for c in (0, 1):
        turn_ref[c] = across(locs_ref[c : c + 1, at])
    def fill_part(first, last):
        for b in range(first // BLOCK, last // BLOCK):
            s = slice(b * BLOCK, (b + 1) * BLOCK)
            value = exp_distance(turn_ref[0, mine, :] - row_locs_ref[0:1, s], turn_ref[1, mine, :] - row_locs_ref[1:2, s])
            part_ref[:, s] = value - prior_ref[:, s]

    fill_part(0, tile)
    pl.semaphore_wait(barrier, jnp.where(alone, 8, 9))

    def cut(ref, index, size, half):
        if half is None:
            return ref.at[pl.ds(pl.multiple_of(index * size, size), size), :]
        return ref.at[pl.ds(pl.multiple_of(index * size + half * (size // 2), size // 2), size // 2), :]

    def slice_of(c, half=None):
        return cut(panel_ref, c, width, half)

    def piece_of(r, half=None):
        return cut(tile_ref, r, width, half)

    sent = []

    def send(of, sends, recvs, index, half, to, src=None):
        slot = sum(1 for entry in sent if entry[1] is sends)
        sent.append((of, sends, slot, half))
        dst = of(index, half)
        pltpu.make_async_remote_copy(
            src_ref=dst if src is None else src,
            dst_ref=dst,
            send_sem=sends.at[slot],
            recv_sem=recvs.at[index, half or 0],
            device_id=to,
            device_id_type=MESH,
        ).start()

    def send_slice(c, to_col, half=None, src=None):
        send(slice_of, slice_send, slice_recv, c, half, (row, to_col), src)

    def send_piece(r, to_row, half=None):
        send(piece_of, piece_send, piece_recv, r, half, (to_row, col))

    def wait_bytes(ref, sem):
        pltpu.make_async_copy(ref, ref, sem).wait()

    def arrived(of, recvs, index, half=None):
        wait_bytes(of(index, half), recvs.at[index, half or 0])

    own_copy = pltpu.make_async_copy(part_ref, slice_of(col), own_sem)
    swap_src = part_ref.at[:, 0:tile]
    locs_src = row_locs_ref.at[:, 0:tile]
    swap_copy = pltpu.make_async_remote_copy(src_ref=swap_src, dst_ref=piece_of(swap_to[0]), send_sem=swap_send.at[0], recv_sem=piece_recv.at[swap_to[0], 0], device_id=swap_to, device_id_type=MESH)
    locs_copy = pltpu.make_async_remote_copy(src_ref=locs_src, dst_ref=col_locs_ref, send_sem=swap_send.at[1], recv_sem=locs_recv, device_id=swap_to, device_id_type=MESH)

    @pl.when(jnp.logical_not(alone))
    def _():
        swap_copy.start()
        locs_copy.start()

    @pl.when(alone)
    def _():
        pltpu.make_async_copy(swap_src, piece_of(row), piece_recv.at[row, 0]).start()
        pltpu.make_async_copy(locs_src, col_locs_ref, locs_recv).start()

    fill_part(tile, rows)
    send_slice(col, partner, src=part_ref)
    half_rows = [part_ref.at[pl.ds(h * (width // 2), width // 2), :] for h in (0, 1)]
    for h in (0, 1):
        send_slice(col, y_own[1], half=h, src=half_rows[h])
        send_slice(col, y_own[0], half=1 - h, src=half_rows[1 - h])
    send_slice(col, sibling, src=part_ref)
    own_copy.start()

    def tile_on():
        arrived(piece_of, piece_recv, row)
        for r in z_rows[:2] + x_rows[:2]:
            send_piece(row, r)

    def partner_to_y():
        arrived(slice_of, slice_recv, partner)
        for h in (0, 1):
            send_slice(partner, y_own[1], half=h)
            send_slice(partner, y_own[0], half=1 - h)
        send_slice(partner, sibling)

    def pass_on(sources):
        for h in (0, 1):
            arrived(slice_of, slice_recv, sources[h], h)
            send_slice(sources[h], y_own[1 - h], half=h)

    def to_sibling(sources):
        for h in (0, 1):
            arrived(slice_of, slice_recv, sources[h], 1 - h)
            send_slice(sources[h], sibling)

    def opposite_slice(c):
        for h in (0, 1):
            arrived(slice_of, slice_recv, c, h)
        send_slice(c, sibling)

    def pieces_on():
        for h in (0, 1):
            arrived(piece_of, piece_recv, z_rows[h])
            send_piece(z_rows[h], z_rows[1 - h], half=h)
            for r in x_rows[:2]:
                send_piece(z_rows[h], r)

    def opposite_piece():
        for h in (0, 1):
            arrived(piece_of, piece_recv, z_rows[2], h)
        for r in x_rows[:2]:
            send_piece(z_rows[2], r)

    def pair_of(b, half):
        return cut(tile_ref, b, 4 * width, half)

    def tiles_on():
        for h in (0, 1):
            for e in range(4):
                arrived(piece_of, piece_recv, x_near[h] * 4 + e)
            send(pair_of, pair_send, pair_recv, x_near[h], h, (x_rows[1 - h], col))

    schedule = [(3, "own"), (4, "tile_on"), (5, "partner_to_y"), (6, "own_over"), (8, "pieces_on"), (8, "opposite_own"), (10, "far"), (11, "opposite_piece"), (12, "far_over"), (13, "tiles_on"), (15, "opposite_far")]
    tasks = dict(
        tile_on=tile_on,
        partner_to_y=partner_to_y,
        own=lambda: pass_on(y_own),
        own_over=lambda: to_sibling(y_own),
        far=lambda: pass_on(y_far),
        far_over=lambda: to_sibling(y_far),
        opposite_own=lambda: opposite_slice(y_own[2]),
        opposite_far=lambda: opposite_slice(y_far[2]),
        pieces_on=pieces_on,
        opposite_piece=opposite_piece,
        tiles_on=tiles_on,
    )
    stages = {}
    for stage, name in schedule:
        stages.setdefault(stage, []).append(tasks[name])

    fill_matrix(locs_ref, m_ref, n, 0)

    def hand_over(first, last):
        def at_strip(k, part):
            for stage in range(first * POINTS + part, last * POINTS, POINTS):
                if stage in stages:
                    @pl.when(k == stage // POINTS)
                    def _():
                        for task in stages[stage]:
                            task()

        return at_strip

    def beside(k, place):
        b = jnp.minimum((k - 1) * len(BESIDE) + place, rows // BLOCK - 1)
        fill_gap(b, row == col, row_locs_ref, col_locs_ref, trail_buf, gap_ref)

    def fill_beside(k, place):
        if place + 1 < blocks:
            fill_matrix(locs_ref, m_ref, n, place + 1)

    invert_step(0, blocks, m_ref, d_ref, inv_ref, hand_over(0, 1), fill_beside)
    wait_bytes(col_locs_ref, locs_recv)
    for part in range(TRAIL_PARTS):
        trail_copy(trail_ref, trail_buf, trail_sems, part).wait()

    def one_block(k, carry):
        invert_step(k, blocks, m_ref, d_ref, inv_ref, hand_over(1, blocks), beside)
        return carry

    lax.fori_loop(1, blocks, one_block, 0)
    for stage in sorted(stages):
        if stage >= POINTS * blocks:
            for task in stages[stage]:
                task()

    for a in range(2):
        for b in range(4):
            arrived(slice_of, slice_recv, col_of(a, b, 1 - core))
    for h in (0, 1):
        wait_bytes(pair_of(x_near[2], h), pair_recv.at[x_near[2], h])
    own_copy.wait()
    for of, sends, slot, half in sent:
        wait_bytes(of(0, half), sends.at[slot])

    @pl.when(jnp.logical_not(alone))
    def _():
        swap_copy.wait_send()
        locs_copy.wait_send()


def gather_and_invert(panel_locs, row_locs, prior_t, prior_trail):
    n = panel_locs.shape[1]
    width, rows = prior_t.shape
    n_col = n // width
    tile = prior_trail.shape[1]
    vmem = pl.BlockSpec(memory_space=pltpu.VMEM)
    anywhere = pl.BlockSpec(memory_space=pl.ANY)
    dma = pltpu.SemaphoreType.DMA
    return pl.pallas_call(
        gather_kernel,
        out_shape=(
            jax.ShapeDtypeStruct((n, rows), f32),
            jax.ShapeDtypeStruct((n, tile), f32),
            jax.ShapeDtypeStruct((n, n), f32),
            jax.ShapeDtypeStruct((rows, tile), f32),
        ),
        in_specs=[pl.BlockSpec(memory_space=pltpu.HBM)] * 4,
        out_specs=(vmem, vmem, vmem, vmem),
        scratch_shapes=[
            pltpu.VMEM((n, n), f32),
            pltpu.VMEM((BLOCK, BLOCK), f32),
            pltpu.VMEM((width, rows), f32),
            pltpu.VMEM((2, BLOCK, BLOCK), f32),
            pltpu.VMEM((rows, tile), f32),
            pltpu.VMEM((2, tile), f32),
            pltpu.VMEM((2, n), f32),
            pltpu.VMEM((2, rows), f32),
            pltpu.VMEM((width, rows), f32),
            dma((TRAIL_PARTS,)),
            dma((3,)),
            dma((21,)), dma((n_col, 2)), dma((12,)), dma((n_col, 2)), dma((2,)), dma((4, 2)), dma((2,)), dma, dma,
        ],
        compiler_params=pltpu.CompilerParams(vmem_limit_bytes=VMEM_A, collective_id=0, has_side_effects=True),
        cost_estimate=pl.CostEstimate(flops=2 * n**3, bytes_accessed=8 * n * n, transcendentals=n * n),
        name="gather_and_invert",
    )(panel_locs, row_locs, prior_t, prior_trail)


def body(row_locs, panel_locs, prior_panel, prior_trail):
    inputs = [pltpu.with_memory_space_constraint(a, pltpu.HBM) for a in (panel_locs, row_locs, prior_panel.T, prior_trail)]
    return trailing_update(*gather_and_invert(*inputs))


def solution(mesh):
    in_specs = (P(None, "row"), P(), P("row", "col"), P("row", "col"))
    out_specs = (P("row", None), P("row", "col"))
    return jax.shard_map(body, mesh=mesh, in_specs=in_specs, out_specs=out_specs, check_vma=False)
```

```python
import jax
import jax.numpy as jnp
from jax import lax
from jax.experimental import pallas as pl
from jax.experimental.pallas import tpu as pltpu
from jax.sharding import PartitionSpec as P

STRIP = 16
AHEAD = 2
HAND_OVER = 1
BLOCK = 128
VMEM_A = 24 * 2**20
VMEM_B = 24 * 2**20
f32, bf16 = jnp.float32, jnp.bfloat16


def exp_distance(dx, dy):
    d2 = dx * dx + dy * dy
    return jnp.exp(d2 * lax.rsqrt(jnp.maximum(d2, 1e-30)) * -10.0)


def split3(x):
    a = x.astype(bf16)
    r = x - a.astype(f32)
    b = r.astype(bf16)
    return a, b, (r - b.astype(f32)).astype(bf16)


def lanes_of(x, j):
    return jnp.broadcast_to(x[:, j : j + 1], (8, BLOCK))


def row_of(x, i):
    return jnp.broadcast_to(x[i : i + 1, :], (8, BLOCK))


def invert_block(d_ref, k, hand_over, beside):
    lane = lax.broadcasted_iota(jnp.int32, (8, BLOCK), 1)
    sub = lax.broadcasted_iota(jnp.int32, (8, BLOCK), 0)
    own = STRIP // 8
    for strip in range(BLOCK // STRIP):
        base = strip * STRIP
        groups = min(own + AHEAD, (BLOCK - base) // 8)
        rows = [d_ref[base + 8 * g : base + 8 * g + 8, :] for g in range(groups)]
        cols = [[lanes_of(rows[g], base + j) for g in range(groups)] for j in range(STRIP)]
        scale = [jnp.zeros((8, BLOCK), f32)] * own
        for i in range(STRIP):
            h, q = i // 8, i % 8
            pivot = row_of(cols[i][h], q)
            inv_pivot = 1.0 / pivot
            scale[h] = jnp.where(sub == q, lax.rsqrt(pivot), scale[h])
            f = [None] * groups
            f[h] = jnp.where(sub > q, cols[i][h], 0.0) * inv_pivot
            for g in range(h + 1, groups):
                f[g] = cols[i][g] * inv_pivot
            for j in range(i + 1, STRIP):
                t = row_of(cols[j][h], q)
                for g in range(h, groups):
                    cols[j][g] = cols[j][g] - f[g] * t
            rows[h] = jnp.where(lane == base + i, jnp.where(sub == q, 1.0, 0.0), rows[h])
            for g in range(h + 1, groups):
                rows[g] = jnp.where(lane == base + i, 0.0, rows[g])
            t = row_of(rows[h], q)
            for g in range(h, groups):
                rows[g] = rows[g] - f[g] * t
        for g in range(own):
            above = (lane > base + 8 * g + sub) & (lane < base + STRIP)
            rows[g] = jnp.where(above, 0.0, rows[g]) * scale[g]
        for g in range(groups):
            d_ref[base + 8 * g : base + 8 * g + 8, :] = rows[g]
        if beside is not None and strip in BESIDE:
            beside(k, BESIDE.index(strip))
        first = base + 8 * groups
        if first < BLOCK:
            a, b, c = split3(jnp.concatenate(rows[:own], axis=0))
            left = jnp.concatenate([a, a, b, a, b, c], axis=0)
            right = jnp.concatenate([a, b, a, c, b, a], axis=0)
            update = lax.dot_general(left, right, (((0,), (0,)), ((), ())), preferred_element_type=f32)
            wide = lax.broadcasted_iota(jnp.int32, (BLOCK - first, BLOCK), 1)
            old = jnp.where((wide >= base) & (wide < base + STRIP), 0.0, d_ref[first:, :])
            d_ref[first:, :] = old - update[first:, :]
        if strip % HAND_OVER == HAND_OVER - 1:
            hand_over(k, strip // HAND_OVER)


def hdot(a, b, dims):
    return lax.dot_general(a, b, (dims, ((), ())), precision=lax.Precision.HIGHEST, preferred_element_type=f32)


def fill_matrix(locs_ref, m_ref, n, bi):
    blocks = n // BLOCK
    eye = lax.broadcasted_iota(jnp.int32, (BLOCK, BLOCK), 0) == lax.broadcasted_iota(jnp.int32, (BLOCK, BLOCK), 1)
    col = [jnp.transpose(jnp.broadcast_to(locs_ref[c : c + 1, bi * BLOCK : (bi + 1) * BLOCK], (BLOCK, BLOCK))) for c in (0, 1)]
    for bj in range(blocks):
        at = (slice(bi * BLOCK, (bi + 1) * BLOCK), slice(bj * BLOCK, (bj + 1) * BLOCK))
        if bj < bi:
            m_ref[at] = jnp.zeros((BLOCK, BLOCK), f32)
            continue
        row = [locs_ref[c : c + 1, bj * BLOCK : (bj + 1) * BLOCK] for c in (0, 1)]
        value = exp_distance(col[0] - row[0], col[1] - row[1])
        if bi == bj:
            value = value + jnp.where(eye, 0.1, 0.0)
        m_ref[at] = value


ROW_TILE = 256


def split2(x):
    high = x.astype(bf16)
    return high, (x - high.astype(f32)).astype(bf16)


def dot3(left, right):
    def one(a, b):
        return lax.dot_general(a, b, (((1,), (1,)), ((), ())), preferred_element_type=f32)

    return one(left[0], right[0]) + (one(left[0], right[1]) + one(left[1], right[0]))


def across(row):
    return jnp.transpose(jnp.broadcast_to(row, (BLOCK, BLOCK)))


def times_lower(left, inv_h, inv_l):
    half = inv_h.shape[0] // 2
    high, low = split2(left)
    top = dot3((high[:, :half], low[:, :half]), (inv_h[:half, :half], inv_l[:half, :half]))
    bottom = dot3((high, low), (inv_h[half:, :], inv_l[half:, :]))
    return jnp.concatenate([top, bottom], axis=1)


def trailing_kernel(panel_ref, tile_ref, inv_h, inv_l, gap_ref, factor_ref, out_ref, factor_buf, out_buf, col_h, col_l, sems):
    rows = panel_ref.shape[1]
    col_h[...], col_l[...] = split2(times_lower(jnp.transpose(tile_ref[...]), inv_h, inv_l))

    def out_copy(buf, ref, which, i):
        at = pl.ds(i * ROW_TILE, ROW_TILE)
        return pltpu.make_async_copy(buf.at[at, :], ref.at[at, :], sems.at[which, i])

    for i in range(rows // ROW_TILE):
        at = slice(i * ROW_TILE, (i + 1) * ROW_TILE)
        factor = times_lower(jnp.transpose(panel_ref[:, at]), inv_h, inv_l)
        factor_buf[at, :] = factor
        out_copy(factor_buf, factor_ref, 0, i).start()
        update = dot3(split2(factor), (col_h[...], col_l[...]))
        out_buf[at, :] = gap_ref[at, :] - update
        out_copy(out_buf, out_ref, 1, i).start()
    for i in range(rows // ROW_TILE):
        out_copy(factor_buf, factor_ref, 0, i).wait()
        out_copy(out_buf, out_ref, 1, i).wait()


def trailing_update(panel_t, tile_t, inv_high, inv_low, gap):
    depth, rows = panel_t.shape
    width = gap.shape[1]
    vmem = pl.BlockSpec(memory_space=pltpu.VMEM)
    anywhere = pl.BlockSpec(memory_space=pl.ANY)
    return pl.pallas_call(
        trailing_kernel,
        out_shape=(jax.ShapeDtypeStruct((rows, depth), f32), jax.ShapeDtypeStruct((rows, width), f32)),
        in_specs=[vmem] * 5,
        out_specs=(anywhere, anywhere),
        scratch_shapes=[
            pltpu.VMEM((rows, depth), f32),
            pltpu.VMEM((rows, width), f32),
            pltpu.VMEM((width, depth), bf16),
            pltpu.VMEM((width, depth), bf16),
            pltpu.SemaphoreType.DMA((2, rows // ROW_TILE)),
        ],
        compiler_params=pltpu.CompilerParams(vmem_limit_bytes=VMEM_B),
        cost_estimate=pl.CostEstimate(flops=12 * rows * depth * width, bytes_accessed=16 * rows * width, transcendentals=0),
        name="trailing_update",
    )(panel_t, tile_t, inv_high, inv_low, gap)


MESH = pl.DeviceIdType.MESH


def invert_step(k, blocks, m_ref, d_ref, inv_h, inv_l, hand_over, beside):
    n = m_ref.shape[1]
    lower = lax.broadcasted_iota(jnp.int32, (BLOCK, BLOCK), 0) >= lax.broadcasted_iota(jnp.int32, (BLOCK, BLOCK), 1)
    lane_block = lax.broadcasted_iota(jnp.int32, (BLOCK, n), 1) // BLOCK
    mine = pl.ds(pl.multiple_of(k * BLOCK, BLOCK), BLOCK)
    d_ref[...] = m_ref[mine, mine]
    invert_block(d_ref, k, hand_over, beside)
    w = jnp.where(lower, d_ref[...], 0.0)
    m_ref[mine, :] = hdot(w, m_ref[mine, :], ((1,), (0,)))
    m_ref[mine, mine] = w
    row = m_ref[mine, :]
    inv_h[mine, :], inv_l[mine, :] = split2(jnp.where(lane_block <= k, row, 0.0))

    def below(i, carry):
        his = pl.ds(pl.multiple_of(i * BLOCK, BLOCK), BLOCK)
        update = hdot(m_ref[mine, his], row, ((0,), (0,)))
        m_ref[his, :] = jnp.where(lane_block == k, 0.0, m_ref[his, :]) - update
        return carry

    lax.fori_loop(k + 1, blocks, below, 0)


TRAIL_PARTS = 4
POINTS = BLOCK // STRIP // HAND_OVER
BESIDE = (0, 1, 3, 4, 6, 7)


def trail_copy(trail_ref, trail_buf, trail_sems, part):
    size = trail_buf.shape[0] // TRAIL_PARTS
    at = pl.ds(part * size, size)
    return pltpu.make_async_copy(trail_ref.at[at, :], trail_buf.at[at, :], trail_sems.at[part])


def fill_gap(b, same, row_locs_ref, col_locs_ref, trail_buf, gap_ref):
    rows = pl.ds(pl.multiple_of(b * BLOCK, BLOCK), BLOCK)
    width = gap_ref.shape[1]
    xr, yr = across(row_locs_ref[0:1, rows]), across(row_locs_ref[1:2, rows])
    i = lax.broadcasted_iota(jnp.int32, (BLOCK, BLOCK), 0) + b * BLOCK
    for block in range(width // BLOCK):
        cols = slice(block * BLOCK, (block + 1) * BLOCK)
        value = exp_distance(xr - col_locs_ref[0:1, cols], yr - col_locs_ref[1:2, cols])
        j = lax.broadcasted_iota(jnp.int32, (BLOCK, BLOCK), 1) + block * BLOCK
        value = value + jnp.where((i == j) & same, 0.1, 0.0)
        gap_ref[rows, cols] = value - trail_buf[rows, cols]


def piece_column(row, col):
    turn = lax.rem(row + 16 - col, 16)
    return lax.rem(turn, 2) * 8 + lax.div(turn, 4) * 2 + lax.rem(lax.div(turn, 2), 2)


def gather_kernel(
    locs_hbm, row_locs_hbm, prior_hbm, trail_ref,
    panel_ref, tile_ref, inv_h, inv_l, gap_ref,
    m_ref, d_ref, part_ref, turn_ref, trail_buf, col_locs_ref, locs_ref, row_locs_ref, prior_ref, trail_sems, in_sems,
    slice_send, slice_recv, piece_send, piece_recv, swap_send, locs_recv, own_sem,
):
    n = locs_ref.shape[1]
    width, rows = prior_ref.shape
    tile = col_locs_ref.shape[1]
    blocks = n // BLOCK
    row, col = lax.axis_index("row"), lax.axis_index("col")
    x, z_hi = lax.div(row, 4), lax.rem(row, 4)
    z_lo, y, core = lax.div(col, 8), lax.rem(lax.div(col, 2), 4), lax.rem(col, 2)

    def near(i):
        return [lax.rem(i + d, 4) for d in (3, 1, 2)]

    def col_of(a, b, c):
        return a * 8 + b * 2 + c

    sibling = col_of(z_lo, y, 1 - core)
    partner = col_of(1 - z_lo, y, core)
    y_own = [col_of(z_lo, b, core) for b in near(y)]
    y_far = [col_of(1 - z_lo, b, core) for b in near(y)]
    z_rows = [x * 4 + b for b in near(z_hi)]
    x_near = near(x)
    x_rows = [b * 4 + z_hi for b in x_near]

    swap_to = (lax.rem(y * 4 + core * 2 + z_lo + row, 16), row)
    swap_from = (col, piece_column(row, col))
    alone = row + col == 0

    loads = [
        pltpu.make_async_copy(src, dst, in_sems.at[i])
        for i, (src, dst) in enumerate([(locs_hbm, locs_ref), (row_locs_hbm, row_locs_ref), (prior_hbm, prior_ref)])
    ]
    for copy in loads:
        copy.start()
    barrier = pltpu.get_barrier_semaphore()
    for b in range(TRAIL_PARTS):
        trail_copy(trail_ref, trail_buf, trail_sems, b).start()
    for c in [sibling, partner] + y_own[:2]:
        pl.semaphore_signal(barrier, inc=1, device_id=(row, c), device_id_type=MESH)
    for r in z_rows + x_rows[:2]:
        pl.semaphore_signal(barrier, inc=1, device_id=(r, col), device_id_type=MESH)

    @pl.when(jnp.logical_not(alone))
    def _():
        pl.semaphore_signal(barrier, inc=1, device_id=swap_from, device_id_type=MESH)

    for copy in loads:
        copy.wait()

    at = pl.ds(pl.multiple_of(lax.div(col, 4) * BLOCK, BLOCK), BLOCK)
    mine = pl.ds(pl.multiple_of(lax.rem(col, 4) * width, width), width)
    for c in (0, 1):
        turn_ref[c] = across(locs_ref[c : c + 1, at])
    def fill_part(first, last):
        for b in range(first // BLOCK, last // BLOCK):
            s = slice(b * BLOCK, (b + 1) * BLOCK)
            value = exp_distance(turn_ref[0, mine, :] - row_locs_ref[0:1, s], turn_ref[1, mine, :] - row_locs_ref[1:2, s])
            part_ref[:, s] = value - prior_ref[:, s]

    fill_part(0, tile)
    pl.semaphore_wait(barrier, jnp.where(alone, 9, 10))

    def cut(ref, index, size, half):
        if half is None:
            return ref.at[pl.ds(pl.multiple_of(index * size, size), size), :]
        return ref.at[pl.ds(pl.multiple_of(index * size + half * (size // 2), size // 2), size // 2), :]

    def slice_of(c, half=None):
        return cut(panel_ref, c, width, half)

    def piece_of(r, half=None):
        return cut(tile_ref, piece_column(r, col), width, half)

    sent = []

    def send(of, sends, recvs, index, half, to, src=None):
        slot = sum(1 for entry in sent if entry[1] is sends)
        sent.append((of, sends, slot, half))
        dst = of(index, half)
        pltpu.make_async_remote_copy(
            src_ref=dst if src is None else src,
            dst_ref=dst,
            send_sem=sends.at[slot],
            recv_sem=recvs.at[index, half or 0],
            device_id=to,
            device_id_type=MESH,
        ).start()

    def send_slice(c, to_col, half=None, src=None):
        send(slice_of, slice_send, slice_recv, c, half, (row, to_col), src)

    def send_piece(r, to_row, half=None):
        send(piece_of, piece_send, piece_recv, r, half, (to_row, col))

    def wait_bytes(ref, sem):
        pltpu.make_async_copy(ref, ref, sem).wait()

    def arrived(of, recvs, index, half=None):
        wait_bytes(of(index, half), recvs.at[index, half or 0])

    own_copy = pltpu.make_async_copy(part_ref, slice_of(col), own_sem)
    swap_src = part_ref.at[:, 0:tile]
    locs_src = row_locs_ref.at[:, 0:tile]
    swap_copy = pltpu.make_async_remote_copy(src_ref=swap_src, dst_ref=cut(tile_ref, col, width, None), send_sem=swap_send.at[0], recv_sem=piece_recv.at[swap_to[0], 0], device_id=swap_to, device_id_type=MESH)
    locs_copy = pltpu.make_async_remote_copy(src_ref=locs_src, dst_ref=col_locs_ref, send_sem=swap_send.at[1], recv_sem=locs_recv, device_id=swap_to, device_id_type=MESH)

    @pl.when(jnp.logical_not(alone))
    def _():
        swap_copy.start()
        locs_copy.start()

    @pl.when(alone)
    def _():
        pltpu.make_async_copy(swap_src, piece_of(row), piece_recv.at[row, 0]).start()
        pltpu.make_async_copy(locs_src, col_locs_ref, locs_recv).start()

    fill_part(tile, rows)
    send_slice(col, partner, src=part_ref)
    half_rows = [part_ref.at[pl.ds(h * (width // 2), width // 2), :] for h in (0, 1)]
    for h in (0, 1):
        send_slice(col, y_own[1], half=h, src=half_rows[h])
        send_slice(col, y_own[0], half=1 - h, src=half_rows[1 - h])
    send_slice(col, sibling, src=part_ref)
    own_copy.start()

    def tile_on():
        arrived(piece_of, piece_recv, row)
        for r in z_rows[:3] + x_rows[:2]:
            send_piece(row, r)

    def partner_to_y():
        arrived(slice_of, slice_recv, partner)
        for h in (0, 1):
            send_slice(partner, y_own[1], half=h)
            send_slice(partner, y_own[0], half=1 - h)
        send_slice(partner, sibling)

    def pass_on(sources):
        for h in (0, 1):
            arrived(slice_of, slice_recv, sources[h], h)
            send_slice(sources[h], y_own[1 - h], half=h)

    def to_sibling(sources):
        for h in (0, 1):
            arrived(slice_of, slice_recv, sources[h], 1 - h)
            send_slice(sources[h], sibling)

    def opposite_own():
        for h in (0, 1):
            arrived(slice_of, slice_recv, y_own[2], h)
        send_slice(y_own[2], partner)
        send_slice(y_own[2], sibling)

    def far_over():
        for h in (0, 1):
            for part in (h, 1 - h):
                arrived(slice_of, slice_recv, y_far[h], part)
            send_slice(y_far[h], sibling)

    def opposite_far():
        arrived(slice_of, slice_recv, y_far[2])
        send_slice(y_far[2], sibling)

    def across_x(zs):
        for z in zs:
            for h in (0, 1):
                arrived(piece_of, piece_recv, x_near[h] * 4 + z)
                send_piece(x_near[h] * 4 + z, x_rows[1 - h], half=h)

    def pieces_on():
        for h in (0, 1):
            arrived(piece_of, piece_recv, z_rows[h])
            for r in x_rows[:2]:
                send_piece(z_rows[h], r)

    def opposite_piece():
        arrived(piece_of, piece_recv, z_rows[2])
        for r in x_rows[:2]:
            send_piece(z_rows[2], r)
        across_x([z_hi])

    schedule = [(6, "own"), (7, "tile_on"), (10, "partner_to_y"), (10, "own_over"), (13, "pieces_on"), (14, "opposite_own"), (16, "opposite_piece"), (20, "far_over"), (20, "tiles_on"), (24, "opposite_far")]
    tasks = dict(
        tile_on=tile_on,
        partner_to_y=partner_to_y,
        own=lambda: pass_on(y_own),
        own_over=lambda: to_sibling(y_own),
        far_over=far_over,
        opposite_own=opposite_own,
        opposite_far=opposite_far,
        pieces_on=pieces_on,
        opposite_piece=opposite_piece,
        tiles_on=lambda: across_x(near(z_hi)),
    )
    stages = {}
    for stage, name in schedule:
        stages.setdefault(stage, []).append(tasks[name])

    fill_matrix(locs_ref, m_ref, n, 0)

    def hand_over(first, last):
        def at_strip(k, part):
            for stage in range(first * POINTS + part, last * POINTS, POINTS):
                if stage in stages:
                    @pl.when(k == stage // POINTS)
                    def _():
                        for task in stages[stage]:
                            task()

        return at_strip

    def beside(k, place):
        b = jnp.minimum((k - 1) * len(BESIDE) + place, rows // BLOCK - 1)
        fill_gap(b, row == col, row_locs_ref, col_locs_ref, trail_buf, gap_ref)

    def fill_beside(k, place):
        if place + 1 < blocks:
            fill_matrix(locs_ref, m_ref, n, place + 1)

    invert_step(0, blocks, m_ref, d_ref, inv_h, inv_l, hand_over(0, 1), fill_beside)
    wait_bytes(col_locs_ref, locs_recv)
    for part in range(TRAIL_PARTS):
        trail_copy(trail_ref, trail_buf, trail_sems, part).wait()

    def one_block(k, carry):
        invert_step(k, blocks, m_ref, d_ref, inv_h, inv_l, hand_over(1, blocks), beside)
        return carry

    lax.fori_loop(1, blocks, one_block, 0)
    for stage in sorted(stages):
        if stage >= POINTS * blocks:
            for task in stages[stage]:
                task()

    for a in range(2):
        for b in range(4):
            arrived(slice_of, slice_recv, col_of(a, b, 1 - core))
    for z in range(4):
        for h in (0, 1):
            arrived(piece_of, piece_recv, x_near[2] * 4 + z, h)
    own_copy.wait()
    for of, sends, slot, half in sent:
        wait_bytes(of(0, half), sends.at[slot])

    @pl.when(jnp.logical_not(alone))
    def _():
        swap_copy.wait_send()
        locs_copy.wait_send()


def gather_and_invert(panel_locs, row_locs, prior_t, prior_trail):
    n = panel_locs.shape[1]
    width, rows = prior_t.shape
    n_col = n // width
    tile = prior_trail.shape[1]
    vmem = pl.BlockSpec(memory_space=pltpu.VMEM)
    anywhere = pl.BlockSpec(memory_space=pl.ANY)
    dma = pltpu.SemaphoreType.DMA
    return pl.pallas_call(
        gather_kernel,
        out_shape=(
            jax.ShapeDtypeStruct((n, rows), f32),
            jax.ShapeDtypeStruct((n, tile), f32),
            jax.ShapeDtypeStruct((n, n), bf16),
            jax.ShapeDtypeStruct((n, n), bf16),
            jax.ShapeDtypeStruct((rows, tile), f32),
        ),
        in_specs=[pl.BlockSpec(memory_space=pltpu.HBM)] * 4,
        out_specs=(vmem,) * 5,
        scratch_shapes=[
            pltpu.VMEM((n, n), f32),
            pltpu.VMEM((BLOCK, BLOCK), f32),
            pltpu.VMEM((width, rows), f32),
            pltpu.VMEM((2, BLOCK, BLOCK), f32),
            pltpu.VMEM((rows, tile), f32),
            pltpu.VMEM((2, tile), f32),
            pltpu.VMEM((2, n), f32),
            pltpu.VMEM((2, rows), f32),
            pltpu.VMEM((width, rows), f32),
            dma((TRAIL_PARTS,)),
            dma((3,)),
            dma((20,)), dma((n_col, 2)), dma((19,)), dma((n_col, 2)), dma((2,)), dma, dma,
        ],
        compiler_params=pltpu.CompilerParams(vmem_limit_bytes=VMEM_A, collective_id=0, has_side_effects=True),
        cost_estimate=pl.CostEstimate(flops=2 * n**3, bytes_accessed=8 * n * n, transcendentals=n * n),
        name="gather_and_invert",
    )(panel_locs, row_locs, prior_t, prior_trail)


def body(row_locs, panel_locs, prior_panel, prior_trail):
    inputs = [pltpu.with_memory_space_constraint(a, pltpu.HBM) for a in (panel_locs, row_locs, prior_panel.T, prior_trail)]
    return trailing_update(*gather_and_invert(*inputs))


def solution(mesh):
    in_specs = (P(None, "row"), P(), P("row", "col"), P("row", "col"))
    out_specs = (P("row", None), P("row", "col"))
    return jax.shard_map(body, mesh=mesh, in_specs=in_specs, out_specs=out_specs, check_vma=False)
```

```python
import jax
import jax.numpy as jnp
from jax import lax
from jax.experimental import pallas as pl
from jax.experimental.pallas import tpu as pltpu
from jax.sharding import PartitionSpec as P

STRIP = 16
AHEAD = 2
HAND_OVER = 2
BLOCK = 128
VMEM_A = 24 * 2**20
VMEM_B = 24 * 2**20
f32, bf16 = jnp.float32, jnp.bfloat16


def exp_distance(dx, dy):
    d2 = dx * dx + dy * dy
    return jnp.exp(d2 * lax.rsqrt(jnp.maximum(d2, 1e-30)) * -10.0)


def split3(x):
    a = x.astype(bf16)
    r = x - a.astype(f32)
    b = r.astype(bf16)
    return a, b, (r - b.astype(f32)).astype(bf16)


def lanes_of(x, j):
    return jnp.broadcast_to(x[:, j : j + 1], (8, BLOCK))


def row_of(x, i):
    return jnp.broadcast_to(x[i : i + 1, :], (8, BLOCK))


def invert_block(d_ref, k, hand_over, beside):
    lane = lax.broadcasted_iota(jnp.int32, (8, BLOCK), 1)
    sub = lax.broadcasted_iota(jnp.int32, (8, BLOCK), 0)
    own = STRIP // 8
    for strip in range(BLOCK // STRIP):
        base = strip * STRIP
        groups = min(own + AHEAD, (BLOCK - base) // 8)
        rows = [d_ref[base + 8 * g : base + 8 * g + 8, :] for g in range(groups)]
        cols = [[lanes_of(rows[g], base + j) for g in range(groups)] for j in range(STRIP)]
        scale = [jnp.zeros((8, BLOCK), f32)] * own
        for i in range(STRIP):
            h, q = i // 8, i % 8
            pivot = row_of(cols[i][h], q)
            inv_pivot = 1.0 / pivot
            scale[h] = jnp.where(sub == q, lax.rsqrt(pivot), scale[h])
            f = [None] * groups
            f[h] = jnp.where(sub > q, cols[i][h], 0.0) * inv_pivot
            for g in range(h + 1, groups):
                f[g] = cols[i][g] * inv_pivot
            for j in range(i + 1, STRIP):
                t = row_of(cols[j][h], q)
                for g in range(h, groups):
                    cols[j][g] = cols[j][g] - f[g] * t
            rows[h] = jnp.where(lane == base + i, jnp.where(sub == q, 1.0, 0.0), rows[h])
            for g in range(h + 1, groups):
                rows[g] = jnp.where(lane == base + i, 0.0, rows[g])
            t = row_of(rows[h], q)
            for g in range(h, groups):
                rows[g] = rows[g] - f[g] * t
        for g in range(own):
            above = (lane > base + 8 * g + sub) & (lane < base + STRIP)
            rows[g] = jnp.where(above, 0.0, rows[g]) * scale[g]
        for g in range(groups):
            d_ref[base + 8 * g : base + 8 * g + 8, :] = rows[g]
        if beside is not None and strip in BESIDE:
            beside(k, BESIDE.index(strip))
        first = base + 8 * groups
        if first < BLOCK:
            a, b, c = split3(jnp.concatenate(rows[:own], axis=0))
            left = jnp.concatenate([a, a, b, a, b, c], axis=0)
            right = jnp.concatenate([a, b, a, c, b, a], axis=0)
            update = lax.dot_general(left, right, (((0,), (0,)), ((), ())), preferred_element_type=f32)
            wide = lax.broadcasted_iota(jnp.int32, (BLOCK - first, BLOCK), 1)
            old = jnp.where((wide >= base) & (wide < base + STRIP), 0.0, d_ref[first:, :])
            d_ref[first:, :] = old - update[first:, :]
        if strip % HAND_OVER == HAND_OVER - 1:
            hand_over(k, strip // HAND_OVER)


def hdot(a, b, dims):
    return lax.dot_general(a, b, (dims, ((), ())), precision=lax.Precision.HIGHEST, preferred_element_type=f32)


def fill_matrix(locs_ref, m_ref, n, bi):
    blocks = n // BLOCK
    eye = lax.broadcasted_iota(jnp.int32, (BLOCK, BLOCK), 0) == lax.broadcasted_iota(jnp.int32, (BLOCK, BLOCK), 1)
    col = [jnp.transpose(jnp.broadcast_to(locs_ref[c : c + 1, bi * BLOCK : (bi + 1) * BLOCK], (BLOCK, BLOCK))) for c in (0, 1)]
    for bj in range(blocks):
        at = (slice(bi * BLOCK, (bi + 1) * BLOCK), slice(bj * BLOCK, (bj + 1) * BLOCK))
        if bj < bi:
            m_ref[at] = jnp.zeros((BLOCK, BLOCK), f32)
            continue
        row = [locs_ref[c : c + 1, bj * BLOCK : (bj + 1) * BLOCK] for c in (0, 1)]
        value = exp_distance(col[0] - row[0], col[1] - row[1])
        if bi == bj:
            value = value + jnp.where(eye, 0.1, 0.0)
        m_ref[at] = value


ROW_TILE = 256


def split2(x):
    high = x.astype(bf16)
    return high, (x - high.astype(f32)).astype(bf16)


def dot3(left, right):
    def one(a, b):
        return lax.dot_general(a, b, (((1,), (1,)), ((), ())), preferred_element_type=f32)

    return one(left[0], right[0]) + (one(left[0], right[1]) + one(left[1], right[0]))


def across(row):
    return jnp.transpose(jnp.broadcast_to(row, (BLOCK, BLOCK)))


def times_lower(left, inv_h, inv_l):
    half = inv_h.shape[0] // 2
    high, low = split2(left)
    top = dot3((high[:, :half], low[:, :half]), (inv_h[:half, :half], inv_l[:half, :half]))
    bottom = dot3((high, low), (inv_h[half:, :], inv_l[half:, :]))
    return jnp.concatenate([top, bottom], axis=1)


def trailing_kernel(panel_ref, tile_ref, inv_h, inv_l, gap_ref, factor_ref, out_ref, factor_buf, out_buf, tile_buf, col_h, col_l, sems):
    rows = panel_ref.shape[1]
    col = lax.axis_index("col")
    piece = tile_ref.shape[0] // 16
    for r in range(16):
        at = pl.ds(pl.multiple_of(piece_column(r, col) * piece, piece), piece)
        tile_buf[at, :] = tile_ref[r * piece : (r + 1) * piece, :]
    col_h[...], col_l[...] = split2(times_lower(jnp.transpose(tile_buf[...]), inv_h, inv_l))

    def out_copy(buf, ref, which, i):
        at = pl.ds(i * ROW_TILE, ROW_TILE)
        return pltpu.make_async_copy(buf.at[at, :], ref.at[at, :], sems.at[which, i])

    for i in range(rows // ROW_TILE):
        at = slice(i * ROW_TILE, (i + 1) * ROW_TILE)
        factor = times_lower(jnp.transpose(panel_ref[:, at]), inv_h, inv_l)
        factor_buf[at, :] = factor
        out_copy(factor_buf, factor_ref, 0, i).start()
        update = dot3(split2(factor), (col_h[...], col_l[...]))
        out_buf[at, :] = gap_ref[at, :] - update
        out_copy(out_buf, out_ref, 1, i).start()
    for i in range(rows // ROW_TILE):
        out_copy(factor_buf, factor_ref, 0, i).wait()
        out_copy(out_buf, out_ref, 1, i).wait()


def trailing_update(panel_t, tile_t, inv_high, inv_low, gap):
    depth, rows = panel_t.shape
    width = gap.shape[1]
    vmem = pl.BlockSpec(memory_space=pltpu.VMEM)
    anywhere = pl.BlockSpec(memory_space=pl.ANY)
    return pl.pallas_call(
        trailing_kernel,
        out_shape=(jax.ShapeDtypeStruct((rows, depth), f32), jax.ShapeDtypeStruct((rows, width), f32)),
        in_specs=[vmem] * 5,
        out_specs=(anywhere, anywhere),
        scratch_shapes=[
            pltpu.VMEM((rows, depth), f32),
            pltpu.VMEM((rows, width), f32),
            pltpu.VMEM((depth, width), f32),
            pltpu.VMEM((width, depth), bf16),
            pltpu.VMEM((width, depth), bf16),
            pltpu.SemaphoreType.DMA((2, rows // ROW_TILE)),
        ],
        compiler_params=pltpu.CompilerParams(vmem_limit_bytes=VMEM_B),
        cost_estimate=pl.CostEstimate(flops=12 * rows * depth * width, bytes_accessed=16 * rows * width, transcendentals=0),
        name="trailing_update",
    )(panel_t, tile_t, inv_high, inv_low, gap)


MESH = pl.DeviceIdType.MESH


def invert_step(k, blocks, m_ref, d_ref, inv_h, inv_l, hand_over, beside):
    n = m_ref.shape[1]
    lower = lax.broadcasted_iota(jnp.int32, (BLOCK, BLOCK), 0) >= lax.broadcasted_iota(jnp.int32, (BLOCK, BLOCK), 1)
    lane_block = lax.broadcasted_iota(jnp.int32, (BLOCK, n), 1) // BLOCK
    mine = pl.ds(pl.multiple_of(k * BLOCK, BLOCK), BLOCK)
    d_ref[...] = m_ref[mine, mine]
    invert_block(d_ref, k, hand_over, beside)
    w = jnp.where(lower, d_ref[...], 0.0)
    m_ref[mine, :] = hdot(w, m_ref[mine, :], ((1,), (0,)))
    m_ref[mine, mine] = w
    row = m_ref[mine, :]
    inv_h[mine, :], inv_l[mine, :] = split2(jnp.where(lane_block <= k, row, 0.0))

    def below(i, carry):
        his = pl.ds(pl.multiple_of(i * BLOCK, BLOCK), BLOCK)
        update = hdot(m_ref[mine, his], row, ((0,), (0,)))
        m_ref[his, :] = jnp.where(lane_block == k, 0.0, m_ref[his, :]) - update
        return carry

    lax.fori_loop(k + 1, blocks, below, 0)


TRAIL_PARTS = 4
POINTS = BLOCK // STRIP // HAND_OVER
BESIDE = (0, 1, 3, 4, 6, 7)


def trail_copy(trail_ref, trail_buf, trail_sems, part):
    size = trail_buf.shape[0] // TRAIL_PARTS
    at = pl.ds(part * size, size)
    return pltpu.make_async_copy(trail_ref.at[at, :], trail_buf.at[at, :], trail_sems.at[part])


def fill_gap(b, same, row_locs_ref, col_locs_ref, trail_buf, gap_ref):
    rows = pl.ds(pl.multiple_of(b * BLOCK, BLOCK), BLOCK)
    width = gap_ref.shape[1]
    xr, yr = across(row_locs_ref[0:1, rows]), across(row_locs_ref[1:2, rows])
    i = lax.broadcasted_iota(jnp.int32, (BLOCK, BLOCK), 0) + b * BLOCK
    for block in range(width // BLOCK):
        cols = slice(block * BLOCK, (block + 1) * BLOCK)
        value = exp_distance(xr - col_locs_ref[0:1, cols], yr - col_locs_ref[1:2, cols])
        j = lax.broadcasted_iota(jnp.int32, (BLOCK, BLOCK), 1) + block * BLOCK
        value = value + jnp.where((i == j) & same, 0.1, 0.0)
        gap_ref[rows, cols] = value - trail_buf[rows, cols]


def piece_column(row, col):
    turn = lax.rem(row + 16 - col, 16)
    return lax.rem(turn, 2) * 8 + lax.div(turn, 4) * 2 + lax.rem(lax.div(turn, 2), 2)


def gather_kernel(
    locs_hbm, row_locs_hbm, prior_hbm, trail_ref,
    panel_ref, tile_ref, inv_h, inv_l, gap_ref,
    m_ref, d_ref, part_ref, turn_ref, trail_buf, col_locs_ref, locs_ref, row_locs_ref, prior_ref, trail_sems, in_sems,
    slice_send, slice_recv, piece_send, piece_recv, pair_send, pair_recv, swap_send, locs_recv, own_sem,
):
    n = locs_ref.shape[1]
    width, rows = prior_ref.shape
    tile = col_locs_ref.shape[1]
    blocks = n // BLOCK
    row, col = lax.axis_index("row"), lax.axis_index("col")
    x, z_hi = lax.div(row, 4), lax.rem(row, 4)
    z_lo, y, core = lax.div(col, 8), lax.rem(lax.div(col, 2), 4), lax.rem(col, 2)

    def near(i):
        return [lax.rem(i + d, 4) for d in (3, 1, 2)]

    def col_of(a, b, c):
        return a * 8 + b * 2 + c

    sibling = col_of(z_lo, y, 1 - core)
    partner = col_of(1 - z_lo, y, core)
    y_own = [col_of(z_lo, b, core) for b in near(y)]
    y_far = [col_of(1 - z_lo, b, core) for b in near(y)]
    z_rows = [x * 4 + b for b in near(z_hi)]
    x_near = near(x)
    x_rows = [b * 4 + z_hi for b in x_near]

    swap_to = (lax.rem(y * 4 + core * 2 + z_lo + row, 16), row)
    swap_from = (col, piece_column(row, col))
    alone = row + col == 0

    loads = [
        pltpu.make_async_copy(src, dst, in_sems.at[i])
        for i, (src, dst) in enumerate([(locs_hbm, locs_ref), (row_locs_hbm, row_locs_ref), (prior_hbm, prior_ref)])
    ]
    for copy in loads:
        copy.start()
    barrier = pltpu.get_barrier_semaphore()
    for b in range(TRAIL_PARTS):
        trail_copy(trail_ref, trail_buf, trail_sems, b).start()
    for c in [sibling, partner] + y_own[:2]:
        pl.semaphore_signal(barrier, inc=1, device_id=(row, c), device_id_type=MESH)
    for r in z_rows[:2] + x_rows[:2]:
        pl.semaphore_signal(barrier, inc=1, device_id=(r, col), device_id_type=MESH)

    @pl.when(jnp.logical_not(alone))
    def _():
        pl.semaphore_signal(barrier, inc=1, device_id=swap_from, device_id_type=MESH)

    for copy in loads:
        copy.wait()

    at = pl.ds(pl.multiple_of(lax.div(col, 4) * BLOCK, BLOCK), BLOCK)
    mine = pl.ds(pl.multiple_of(lax.rem(col, 4) * width, width), width)
    for c in (0, 1):
        turn_ref[c] = across(locs_ref[c : c + 1, at])
    def fill_part(first, last):
        for b in range(first // BLOCK, last // BLOCK):
            s = slice(b * BLOCK, (b + 1) * BLOCK)
            value = exp_distance(turn_ref[0, mine, :] - row_locs_ref[0:1, s], turn_ref[1, mine, :] - row_locs_ref[1:2, s])
            part_ref[:, s] = value - prior_ref[:, s]

    fill_part(0, tile)
    pl.semaphore_wait(barrier, jnp.where(alone, 8, 9))

    def cut(ref, index, size, half):
        if half is None:
            return ref.at[pl.ds(pl.multiple_of(index * size, size), size), :]
        return ref.at[pl.ds(pl.multiple_of(index * size + half * (size // 2), size // 2), size // 2), :]

    def slice_of(c, half=None):
        return cut(panel_ref, c, width, half)

    def piece_of(r, half=None):
        return cut(tile_ref, r, width, half)

    sent = []

    def send(of, sends, recvs, index, half, to, src=None):
        slot = sum(1 for entry in sent if entry[1] is sends)
        sent.append((of, sends, slot, half))
        dst = of(index, half)
        pltpu.make_async_remote_copy(
            src_ref=dst if src is None else src,
            dst_ref=dst,
            send_sem=sends.at[slot],
            recv_sem=recvs.at[index, half or 0],
            device_id=to,
            device_id_type=MESH,
        ).start()

    def send_slice(c, to_col, half=None, src=None):
        send(slice_of, slice_send, slice_recv, c, half, (row, to_col), src)

    def send_piece(r, to_row, half=None):
        send(piece_of, piece_send, piece_recv, r, half, (to_row, col))

    def wait_bytes(ref, sem):
        pltpu.make_async_copy(ref, ref, sem).wait()

    def arrived(of, recvs, index, half=None):
        wait_bytes(of(index, half), recvs.at[index, half or 0])

    own_copy = pltpu.make_async_copy(part_ref, slice_of(col), own_sem)
    swap_src = part_ref.at[:, 0:tile]
    locs_src = row_locs_ref.at[:, 0:tile]
    swap_copy = pltpu.make_async_remote_copy(src_ref=swap_src, dst_ref=piece_of(swap_to[0]), send_sem=swap_send.at[0], recv_sem=piece_recv.at[swap_to[0], 0], device_id=swap_to, device_id_type=MESH)
    locs_copy = pltpu.make_async_remote_copy(src_ref=locs_src, dst_ref=col_locs_ref, send_sem=swap_send.at[1], recv_sem=locs_recv, device_id=swap_to, device_id_type=MESH)

    @pl.when(jnp.logical_not(alone))
    def _():
        swap_copy.start()
        locs_copy.start()

    @pl.when(alone)
    def _():
        pltpu.make_async_copy(swap_src, piece_of(row), piece_recv.at[row, 0]).start()
        pltpu.make_async_copy(locs_src, col_locs_ref, locs_recv).start()

    fill_part(tile, rows)
    send_slice(col, partner, src=part_ref)
    half_rows = [part_ref.at[pl.ds(h * (width // 2), width // 2), :] for h in (0, 1)]
    for h in (0, 1):
        send_slice(col, y_own[1], half=h, src=half_rows[h])
        send_slice(col, y_own[0], half=1 - h, src=half_rows[1 - h])
    send_slice(col, sibling, src=part_ref)
    own_copy.start()

    def tile_on():
        arrived(piece_of, piece_recv, row)
        for r in z_rows[:2] + x_rows[:2]:
            send_piece(row, r)

    def partner_to_y():
        arrived(slice_of, slice_recv, partner)
        for h in (0, 1):
            send_slice(partner, y_own[1], half=h)
            send_slice(partner, y_own[0], half=1 - h)
        send_slice(partner, sibling)

    def pass_on(sources):
        for h in (0, 1):
            arrived(slice_of, slice_recv, sources[h], h)
            send_slice(sources[h], y_own[1 - h], half=h)

    def to_sibling(sources):
        for h in (0, 1):
            arrived(slice_of, slice_recv, sources[h], 1 - h)
            send_slice(sources[h], sibling)

    def opposite_slice(c):
        for h in (0, 1):
            arrived(slice_of, slice_recv, c, h)
        send_slice(c, sibling)

    def pieces_on():
        for h in (0, 1):
            arrived(piece_of, piece_recv, z_rows[h])
            send_piece(z_rows[h], z_rows[1 - h], half=h)
            for r in x_rows[:2]:
                send_piece(z_rows[h], r)

    def opposite_piece():
        for h in (0, 1):
            arrived(piece_of, piece_recv, z_rows[2], h)
        for r in x_rows[:2]:
            send_piece(z_rows[2], r)

    def pair_of(b, half):
        return cut(tile_ref, b, 4 * width, half)

    def tiles_on():
        for h in (0, 1):
            for e in range(4):
                arrived(piece_of, piece_recv, x_near[h] * 4 + e)
            send(pair_of, pair_send, pair_recv, x_near[h], h, (x_rows[1 - h], col))

    schedule = [(3, "own"), (4, "tile_on"), (5, "partner_to_y"), (6, "own_over"), (8, "pieces_on"), (8, "opposite_own"), (10, "far"), (11, "opposite_piece"), (12, "far_over"), (13, "tiles_on"), (15, "opposite_far")]
    tasks = dict(
        tile_on=tile_on,
        partner_to_y=partner_to_y,
        own=lambda: pass_on(y_own),
        own_over=lambda: to_sibling(y_own),
        far=lambda: pass_on(y_far),
        far_over=lambda: to_sibling(y_far),
        opposite_own=lambda: opposite_slice(y_own[2]),
        opposite_far=lambda: opposite_slice(y_far[2]),
        pieces_on=pieces_on,
        opposite_piece=opposite_piece,
        tiles_on=tiles_on,
    )
    stages = {}
    for stage, name in schedule:
        stages.setdefault(stage, []).append(tasks[name])

    fill_matrix(locs_ref, m_ref, n, 0)

    def hand_over(first, last):
        def at_strip(k, part):
            for stage in range(first * POINTS + part, last * POINTS, POINTS):
                if stage in stages:
                    @pl.when(k == stage // POINTS)
                    def _():
                        for task in stages[stage]:
                            task()

        return at_strip

    def beside(k, place):
        b = jnp.minimum((k - 1) * len(BESIDE) + place, rows // BLOCK - 1)
        fill_gap(b, row == col, row_locs_ref, col_locs_ref, trail_buf, gap_ref)

    def fill_beside(k, place):
        if place + 1 < blocks:
            fill_matrix(locs_ref, m_ref, n, place + 1)

    invert_step(0, blocks, m_ref, d_ref, inv_h, inv_l, hand_over(0, 1), fill_beside)
    wait_bytes(col_locs_ref, locs_recv)
    for part in range(TRAIL_PARTS):
        trail_copy(trail_ref, trail_buf, trail_sems, part).wait()

    def one_block(k, carry):
        invert_step(k, blocks, m_ref, d_ref, inv_h, inv_l, hand_over(1, blocks), beside)
        return carry

    lax.fori_loop(1, blocks, one_block, 0)
    for stage in sorted(stages):
        if stage >= POINTS * blocks:
            for task in stages[stage]:
                task()

    for a in range(2):
        for b in range(4):
            arrived(slice_of, slice_recv, col_of(a, b, 1 - core))
    for h in (0, 1):
        wait_bytes(pair_of(x_near[2], h), pair_recv.at[x_near[2], h])
    own_copy.wait()
    for of, sends, slot, half in sent:
        wait_bytes(of(0, half), sends.at[slot])

    @pl.when(jnp.logical_not(alone))
    def _():
        swap_copy.wait_send()
        locs_copy.wait_send()


def gather_and_invert(panel_locs, row_locs, prior_t, prior_trail):
    n = panel_locs.shape[1]
    width, rows = prior_t.shape
    n_col = n // width
    tile = prior_trail.shape[1]
    vmem = pl.BlockSpec(memory_space=pltpu.VMEM)
    anywhere = pl.BlockSpec(memory_space=pl.ANY)
    dma = pltpu.SemaphoreType.DMA
    return pl.pallas_call(
        gather_kernel,
        out_shape=(
            jax.ShapeDtypeStruct((n, rows), f32),
            jax.ShapeDtypeStruct((n, tile), f32),
            jax.ShapeDtypeStruct((n, n), bf16),
            jax.ShapeDtypeStruct((n, n), bf16),
            jax.ShapeDtypeStruct((rows, tile), f32),
        ),
        in_specs=[pl.BlockSpec(memory_space=pltpu.HBM)] * 4,
        out_specs=(vmem,) * 5,
        scratch_shapes=[
            pltpu.VMEM((n, n), f32),
            pltpu.VMEM((BLOCK, BLOCK), f32),
            pltpu.VMEM((width, rows), f32),
            pltpu.VMEM((2, BLOCK, BLOCK), f32),
            pltpu.VMEM((rows, tile), f32),
            pltpu.VMEM((2, tile), f32),
            pltpu.VMEM((2, n), f32),
            pltpu.VMEM((2, rows), f32),
            pltpu.VMEM((width, rows), f32),
            dma((TRAIL_PARTS,)),
            dma((3,)),
            dma((21,)), dma((n_col, 2)), dma((12,)), dma((n_col, 2)), dma((2,)), dma((4, 2)), dma((2,)), dma, dma,
        ],
        compiler_params=pltpu.CompilerParams(vmem_limit_bytes=VMEM_A, collective_id=0, has_side_effects=True),
        cost_estimate=pl.CostEstimate(flops=2 * n**3, bytes_accessed=8 * n * n, transcendentals=n * n),
        name="gather_and_invert",
    )(panel_locs, row_locs, prior_t, prior_trail)


def body(row_locs, panel_locs, prior_panel, prior_trail):
    inputs = [pltpu.with_memory_space_constraint(a, pltpu.HBM) for a in (panel_locs, row_locs, prior_panel.T, prior_trail)]
    return trailing_update(*gather_and_invert(*inputs))


def solution(mesh):
    in_specs = (P(None, "row"), P(), P("row", "col"), P("row", "col"))
    out_specs = (P("row", None), P("row", "col"))
    return jax.shard_map(body, mesh=mesh, in_specs=in_specs, out_specs=out_specs, check_vma=False)
```
